256 devices in a mesh: dp: 32 (over z, y), tensor: 8 (over x, core).
Axes of the slice: x: 4, y: 4, z: 8, core: 2. Of those that a mesh axis runs over, the one named last changes fastest.
Arguments:
- hidden_in: bfloat16 [65536, 14336], P('dp', 'tensor'), may hold values from -6 to 6
- out_grad: bfloat16 [65536, 4096], P('dp', 'tensor'), may hold values from -6 to 6
- proj_in: bfloat16 [14336, 64], P('tensor'), may hold values from -0.046875 to 0.046875
- proj_out: bfloat16 [4096, 64], P('tensor'), may hold values from -0.09375 to 0.09375
- token_mask: int32 [65536], P('dp'), may hold values 0 or 1
- cand_ids: int32 [32], P('dp'), may hold values from 0 to 1023
- queries: bfloat16 [1024, 4096], P('tensor', 'dp'), may hold values from -6 to 6
Outputs:
- scores: float32 [32, 1024], P('dp', 'tensor')
The draws below stay inside these ranges and needn't reach their ends.
All inputs are finite; a program needn't handle non-finite values. No bound on the sum of `token_mask` on one device may be relied on, other than what follows from the above.
Results may differ from the reference program's by a relative error of at most 0.0029.
Values may be sent and summed in bfloat16 or wider, within the bound.
No kernel may reach another device: no remote copies, remote signals or barrier semaphores. Data moves between devices by JAX's collectives and lax.ppermute only.
A program may use at most 64 MiB of HBM per device.

```python
import jax
import jax.numpy as jnp
from jax import lax

D = 4096
FF = 14336
R = 64
RR = 4096
QUERIES = 1024
LEN = 2048
CAND = 32
TOKENS = 65536


def set_ends(array, rng, least, high):
    place = [jax.random.randint(jax.random.fold_in(rng, axis), (), 0, length) for axis, length in enumerate(array.shape)]
    widest = array.shape.index(max(array.shape))
    next_to = place[:widest] + [(place[widest] + 1) % array.shape[widest]] + place[widest + 1:]
    return array.at[tuple(place)].set(least).at[tuple(next_to)].set(high)


def block_levels(rng, dims, shards, low, high):
    level, own = 1.0, jax.random.fold_in(rng, 6)
    for dim, shards_of in shards:
        draws = jnp.exp(jax.random.uniform(jax.random.fold_in(own, dim), (shards_of,), jnp.float32, low / len(shards), high / len(shards)))
        level = level * jnp.repeat(draws, dims[dim] // shards_of).reshape([-1 if axis == dim else 1 for axis in range(len(dims))])
    return level


def noise(own_key, dims, scale, bound, pieces=(), kind=jnp.bfloat16):
    array = jax.random.normal(own_key, dims, jnp.float32) * scale
    if len(pieces) > 0:
        array = block_levels(own_key, dims, pieces, -0.22, 0.18) * array
    return jnp.clip(array, min=-bound, max=bound).astype(kind)


def setup_inputs(seed: int = 0) -> dict:
    arg_keys = jax.random.split(jax.random.key(seed), 8)
    hidden_in = noise(arg_keys[0], (TOKENS, FF), 1.0, 6.0, ((0, 32), (1, 8)))
    out_grad = noise(arg_keys[1], (TOKENS, D), 1.0, 6.0, ((0, 32), (1, 8)))
    proj_in = noise(arg_keys[2], (FF, R), FF ** -0.5, 0.046875, ((0, 8),))
    proj_out = noise(arg_keys[3], (D, R), D ** -0.5, 0.09375, ((0, 8),))
    token_mask = set_ends((jax.random.randint(arg_keys[4], (TOKENS,), 0, 4) < 3).astype(jnp.int32), jax.random.fold_in(arg_keys[4], 1), 0, 1)
    cand_ids = set_ends(jax.random.randint(arg_keys[5], (CAND,), 0, QUERIES), jax.random.fold_in(arg_keys[5], 1), 0, QUERIES - 1).astype(jnp.int32)
    queries = noise(arg_keys[6], (QUERIES, RR), 1.0, 6.0, ((0, 8), (1, 32)))
    return dict(hidden_in=hidden_in, out_grad=out_grad, proj_in=proj_in, proj_out=proj_out, token_mask=token_mask, cand_ids=cand_ids, queries=queries)


def reference(hidden_in, out_grad, proj_in, proj_out, token_mask, cand_ids, queries):
    xp = jnp.dot(hidden_in, proj_in, preferred_element_type=jnp.float32)
    gp = jnp.dot(out_grad, proj_out, preferred_element_type=jnp.float32)
    weighted = gp * token_mask.astype(jnp.float32)[:, None]
    weighted = weighted.reshape(CAND, LEN, R)
    inputs = xp.reshape(CAND, LEN, R)
    grad = jnp.einsum('cti,ctj->cij', weighted, inputs, precision=lax.Precision.HIGHEST)
    flat = grad.reshape(CAND, R * R)
    grms = jnp.sqrt(lax.optimization_barrier(jnp.mean(flat * flat, axis=1, keepdims=True)) + 1e-06)
    unit = (flat / grms).astype(jnp.bfloat16)
    qfloat = queries.astype(jnp.float32)
    qrms = jnp.sqrt(lax.optimization_barrier(jnp.mean(qfloat * qfloat, axis=1)) + 1e-06)
    dots = jnp.dot(unit, queries.T, preferred_element_type=jnp.float32)
    scores = dots / (R * qrms[None, :])
    index = jnp.arange(QUERIES, dtype=jnp.int32)
    return jnp.where(index[None, :] == cand_ids[:, None], jnp.float32(0.0), scores)
```

```python
import functools

import jax
import jax.numpy as jnp
from jax import lax
from jax.experimental import pallas as pl
from jax.experimental.pallas import tpu as pltpu
from jax.sharding import PartitionSpec as P

BLOCK = 256
PROJECT_VMEM = 61 << 20
SMALL_VMEM = 8 << 20
ROWS = 4
HIGHEST = lax.Precision.HIGHEST


def nt_dot(a, b, precision=None):
    return lax.dot_general(
        a, b, (((1,), (1,)), ((), ())), preferred_element_type=jnp.float32, precision=precision
    )


def project_kernel(place_ref, hidden_ref, grad_ref, pin_ref, pout_ref, out_ref, w_ref):
    rank, width = pin_ref.shape

    @pl.when(pl.program_id(0) == 0)
    def _():
        w_ref[...] = jnp.zeros_like(w_ref)
        w_ref[:rank, :width] = pin_ref[...]
        w_ref[rank:, width:] = pout_ref[...]

    out_ref[...] = nt_dot(hidden_ref[...], w_ref[:, :width]) + nt_dot(grad_ref[...], w_ref[:, width:])


def project(place, hidden, grad, pin_t, pout_t):
    rank, width = pin_t.shape
    depth = pout_t.shape[1]
    rows = hidden.shape[0] // 2
    steps = rows // BLOCK

    def tokens(k, place_ref):
        return place_ref[0] * steps + jnp.bitwise_xor(place_ref[1], k), 0

    def whole(k, place_ref):
        return 0, 0

    return pl.pallas_call(
        project_kernel,
        out_shape=jax.ShapeDtypeStruct((rows, 2 * rank), jnp.float32),
        grid_spec=pltpu.PrefetchScalarGridSpec(
            num_scalar_prefetch=1,
            grid=(steps,),
            in_specs=[
                pl.BlockSpec((BLOCK, width), tokens),
                pl.BlockSpec((BLOCK, depth), tokens),
                pl.BlockSpec((rank, width), whole),
                pl.BlockSpec((rank, depth), whole),
            ],
            out_specs=pl.BlockSpec((BLOCK, 2 * rank), lambda k, place_ref: (k, 0)),
            scratch_shapes=[pltpu.VMEM((2 * rank, width + depth), jnp.bfloat16)],
        ),
        compiler_params=pltpu.CompilerParams(vmem_limit_bytes=PROJECT_VMEM),
        cost_estimate=pl.CostEstimate(
            flops=2 * rows * (width + depth) * 256, bytes_accessed=2 * rows * (width + depth), transcendentals=0
        ),
        name="project",
    )(place, hidden, grad, pin_t, pout_t)


def pair_kernel(a_ref, b_ref, *outs):
    for k, out in enumerate(outs):
        rows = pl.ds(k * BLOCK, BLOCK)
        out[...] = a_ref[rows, :] + b_ref[rows, :]


def pair_sum(a, b):
    n = a.shape[0] // BLOCK
    vmem = pl.BlockSpec(memory_space=pltpu.VMEM)
    return pl.pallas_call(
        pair_kernel,
        out_shape=[jax.ShapeDtypeStruct((BLOCK, a.shape[1]), jnp.float32)] * n,
        in_specs=[vmem] * 2,
        out_specs=[vmem] * n,
        compiler_params=pltpu.CompilerParams(vmem_limit_bytes=SMALL_VMEM),
        name="pair_sum",
    )(a, b)


def outer_kernel(first_ref, mask_ref, *refs):
    parts, out_ref, tmp_ref = refs[:-2], refs[-2], refs[-1]
    mask = mask_ref[pl.ds(first_ref[0], 1), :].astype(jnp.float32)
    total = functools.reduce(lambda a, b: a + b, [r[...] for r in parts])
    rank = total.shape[1] // 2
    masked = total.T[rank:, :] * mask
    tmp_ref[...] = lax.dot_general(
        masked, total, (((1,), (0,)), ((), ())), preferred_element_type=jnp.float32, precision=HIGHEST
    )
    even = tmp_ref[pl.ds(0, rank // 2, stride=2), :]
    odd = tmp_ref[pl.ds(1, rank // 2, stride=2), :]
    out_ref[...] = jnp.concatenate([even[:, :rank], odd[:, :rank]], axis=1)


def outer(first, mask, parts):
    vmem = pl.BlockSpec(memory_space=pltpu.VMEM)
    rank = parts[0].shape[1] // 2
    return pl.pallas_call(
        outer_kernel,
        out_shape=jax.ShapeDtypeStruct((rank // 2, 2 * rank), jnp.float32),
        in_specs=[pl.BlockSpec(memory_space=pltpu.SMEM)] + [vmem] * (1 + len(parts)),
        out_specs=vmem,
        scratch_shapes=[pltpu.VMEM((rank, 2 * rank), jnp.float32)],
        compiler_params=pltpu.CompilerParams(vmem_limit_bytes=SMALL_VMEM),
        name="outer",
    )(first, mask, *parts)


def sum_kernel(*refs):
    refs[-1][...] = functools.reduce(lambda a, b: a + b, [r[...] for r in refs[:-1]])


def sum_parts(parts):
    vmem = pl.BlockSpec(memory_space=pltpu.VMEM)
    return pl.pallas_call(
        sum_kernel,
        out_shape=jax.ShapeDtypeStruct(parts[0].shape, jnp.float32),
        in_specs=[vmem] * len(parts),
        out_specs=vmem,
        compiler_params=pltpu.CompilerParams(vmem_limit_bytes=SMALL_VMEM),
        name="sum_parts",
    )(*parts)


def score_kernel(rank, ids_ref, a_ref, b_ref, *refs):
    q_refs, out_ref, unit_ref = refs[:-2], refs[-2], refs[-1]
    grad = a_ref[...] + b_ref[...]
    entries = grad.size
    mean = jnp.sum(grad * grad, keepdims=True) / entries
    unit_ref[...] = (grad / jnp.sqrt(mean + 1e-06)).astype(jnp.bfloat16).astype(jnp.float32)
    layers, qlocal, lanes = q_refs[0].shape
    dots = jnp.zeros((qlocal, lanes), jnp.float32)
    squares = jnp.zeros((qlocal, lanes), jnp.float32)
    for z in range(layers):
        for k, q_ref in enumerate(q_refs):
            q = q_ref[z].astype(jnp.float32)
            row = z * len(q_refs) + jnp.bitwise_xor(ids_ref[2], k)
            dots += q * unit_ref[pl.ds(row, 1), :]
            squares += q * q
    ones = jnp.ones((8, lanes), jnp.float32)
    dots = nt_dot(ones, dots, HIGHEST)[:1]
    squares = nt_dot(ones, squares, HIGHEST)[:1]
    scores = dots / (rank * jnp.sqrt(squares / entries + 1e-06))
    index = ids_ref[1] + lax.broadcasted_iota(jnp.int32, scores.shape, 1)
    out_ref[...] = jnp.where(index == ids_ref[0], 0.0, scores)


def score(rank, ids, a, b, q):
    vmem = pl.BlockSpec(memory_space=pltpu.VMEM)
    return pl.pallas_call(
        functools.partial(score_kernel, rank),
        out_shape=jax.ShapeDtypeStruct((1, q[0].shape[1]), jnp.float32),
        in_specs=[pl.BlockSpec(memory_space=pltpu.SMEM)] + [vmem] * (2 + len(q)),
        out_specs=vmem,
        scratch_shapes=[pltpu.VMEM(a.shape, jnp.float32)],
        compiler_params=pltpu.CompilerParams(vmem_limit_bytes=SMALL_VMEM),
        name="score",
    )(ids, a, b, *q)


def body(hidden_in, out_grad, proj_in, proj_out, token_mask, cand_ids, queries):
    rank = proj_in.shape[1]
    devices = lax.axis_size("tensor")
    chips = devices // 2
    dp = lax.axis_size("dp")
    me = lax.axis_index("tensor").astype(jnp.int32)
    core, chip = me % 2, me // 2
    qlocal, qcols = queries.shape

    def swap(x, mask):
        return lax.ppermute(x, "tensor", [(i, i ^ mask) for i in range(devices)])

    with jax.named_scope("gather_queries"):
        layers = dp // ROWS
        columns = [[z * ROWS + y for z in range(layers)] for y in range(ROWS)]
        copies = jnp.broadcast_to(queries[None], (layers, qlocal, qcols))
        column = lax.all_to_all(copies, "dp", 0, 0, tiled=True, axis_index_groups=columns)
        gathered = [column] + [
            lax.ppermute(column, "dp", [(i, i ^ k) for i in range(dp)]) for k in range(1, ROWS)
        ]

    pin_t, pout_t = proj_in.T, proj_out.T
    with jax.named_scope("project"):
        theirs = project(jnp.stack([1 - core, chip]), hidden_in, out_grad, pin_t, pout_t)
        arrived = swap(theirs, 1)
        mine = project(jnp.stack([core, chip]), hidden_in, out_grad, pin_t, pout_t)
    with jax.named_scope("exchange_tokens"):
        blocks = pair_sum(mine, arrived)
        parts = [blocks[0]] + [swap(blocks[k], 2 * k) for k in range(1, chips)]
    with jax.named_scope("outer"):
        first = (core * chips + chip)[None]
        partial = outer(first, token_mask.reshape(-1, BLOCK), parts)
    with jax.named_scope("exchange_grad"):
        half = sum_parts([partial] + [swap(partial, 2 * k) for k in range(1, chips)])
        other = swap(half, 1)
    with jax.named_scope("score"):
        row = lax.axis_index("dp").astype(jnp.int32) % ROWS
        ids = jnp.stack([cand_ids[0], me * qlocal, row])
        return score(rank, ids, half, other, gathered)


def solution(mesh):
    placed = (
        P("dp", "tensor"),
        P("dp", "tensor"),
        P("tensor", None),
        P("tensor", None),
        P("dp"),
        P("dp"),
        P("tensor", "dp"),
    )
    return jax.shard_map(
        body, mesh=mesh, in_specs=placed, out_specs=P("dp", "tensor"), check_vma=False
    )
```

```python
import functools

import jax
import jax.numpy as jnp
from jax import lax
from jax.experimental import pallas as pl
from jax.experimental.pallas import tpu as pltpu
from jax.sharding import PartitionSpec as P

BLOCK = 256
PROJECT_VMEM = 16 << 20
FIRST_FLOPS = 8 << 30
SMALL_VMEM = 8 << 20
ROWS = 4
NO_COST = pl.CostEstimate(flops=0, bytes_accessed=0, transcendentals=0)
HIGHEST = lax.Precision.HIGHEST


def nt_dot(a, b, precision=None):
    return lax.dot_general(
        a, b, (((1,), (1,)), ((), ())), preferred_element_type=jnp.float32, precision=precision
    )


def copies_kernel(q_ref, out_ref):
    for z in range(out_ref.shape[0]):
        out_ref[z] = q_ref[...]


def copies_of(queries, layers):
    vmem = pl.BlockSpec(memory_space=pltpu.VMEM)
    return pl.pallas_call(
        copies_kernel,
        out_shape=jax.ShapeDtypeStruct((layers, *queries.shape), queries.dtype),
        in_specs=[vmem],
        out_specs=vmem,
        compiler_params=pltpu.CompilerParams(vmem_limit_bytes=SMALL_VMEM),
        cost_estimate=pl.CostEstimate(flops=FIRST_FLOPS, bytes_accessed=1 << 20, transcendentals=0),
        name="copies",
    )(queries)


def project_kernel(place_ref, hidden_ref, grad_ref, pin_ref, pout_ref, *refs):
    outs, w_ref = refs[:-1], refs[-1]
    rank, width = pin_ref.shape
    depth = pout_ref.shape[1]
    w_ref[:rank, :width] = pin_ref[...]
    w_ref[rank:, :width] = jnp.zeros((rank, width), w_ref.dtype)
    w_ref[:rank, width:] = jnp.zeros((rank, depth), w_ref.dtype)
    w_ref[rank:, width:] = pout_ref[...]
    blocks = len(outs) // 2
    for n, out_ref in enumerate(outs):
        half = 1 - place_ref[0] if n < blocks else place_ref[0]
        first = (half * blocks + jnp.bitwise_xor(place_ref[1], n % blocks)) * BLOCK
        rows = pl.ds(pl.multiple_of(first, BLOCK), BLOCK)
        out_ref[...] = nt_dot(hidden_ref[rows, :], w_ref[:, :width]) + nt_dot(grad_ref[rows, :], w_ref[:, width:])


def project(place, hidden, grad, pin_t, pout_t):
    rank, width = pin_t.shape
    blocks = hidden.shape[0] // BLOCK
    vmem = pl.BlockSpec(memory_space=pltpu.VMEM)
    return pl.pallas_call(
        project_kernel,
        out_shape=[jax.ShapeDtypeStruct((BLOCK, 2 * rank), jnp.float32)] * blocks,
        in_specs=[pl.BlockSpec(memory_space=pltpu.SMEM)] + [vmem] * 4,
        out_specs=[vmem] * blocks,
        scratch_shapes=[pltpu.VMEM((2 * rank, width + pout_t.shape[1]), pin_t.dtype)],
        compiler_params=pltpu.CompilerParams(vmem_limit_bytes=PROJECT_VMEM),
        cost_estimate=NO_COST,
        name="project",
    )(place, hidden, grad, pin_t, pout_t)


def pair_kernel(*refs):
    n = len(refs) // 3
    for a_ref, b_ref, out_ref in zip(refs[:n], refs[n : 2 * n], refs[2 * n :]):
        out_ref[...] = a_ref[...] + b_ref[...]


def pair_sum(a, b):
    vmem = pl.BlockSpec(memory_space=pltpu.VMEM)
    return pl.pallas_call(
        pair_kernel,
        out_shape=[jax.ShapeDtypeStruct(x.shape, x.dtype) for x in a],
        in_specs=[vmem] * (2 * len(a)),
        out_specs=[vmem] * len(a),
        compiler_params=pltpu.CompilerParams(vmem_limit_bytes=SMALL_VMEM),
        cost_estimate=NO_COST,
        name="pair_sum",
    )(*a, *b)


def outer_kernel(first_ref, mask_ref, *refs):
    parts, out_ref, tmp_ref = refs[:-2], refs[-2], refs[-1]
    mask = mask_ref[pl.ds(first_ref[0], 1), :].astype(jnp.float32)
    total = functools.reduce(lambda a, b: a + b, [r[...] for r in parts])
    rank = total.shape[1] // 2
    masked = total.T[rank:, :] * mask
    tmp_ref[...] = lax.dot_general(
        masked, total, (((1,), (0,)), ((), ())), preferred_element_type=jnp.float32, precision=HIGHEST
    )
    even = tmp_ref[pl.ds(0, rank // 2, stride=2), :]
    odd = tmp_ref[pl.ds(1, rank // 2, stride=2), :]
    out_ref[...] = jnp.concatenate([even[:, :rank], odd[:, :rank]], axis=1)


def outer(first, mask, parts):
    vmem = pl.BlockSpec(memory_space=pltpu.VMEM)
    rank = parts[0].shape[1] // 2
    return pl.pallas_call(
        outer_kernel,
        out_shape=jax.ShapeDtypeStruct((rank // 2, 2 * rank), jnp.float32),
        in_specs=[pl.BlockSpec(memory_space=pltpu.SMEM)] + [vmem] * (1 + len(parts)),
        out_specs=vmem,
        scratch_shapes=[pltpu.VMEM((rank, 2 * rank), jnp.float32)],
        compiler_params=pltpu.CompilerParams(vmem_limit_bytes=SMALL_VMEM),
        cost_estimate=NO_COST,
        name="outer",
    )(first, mask, *parts)


def sum_kernel(*refs):
    refs[-1][...] = functools.reduce(lambda a, b: a + b, [r[...] for r in refs[:-1]])


def sum_parts(parts):
    vmem = pl.BlockSpec(memory_space=pltpu.VMEM)
    return pl.pallas_call(
        sum_kernel,
        out_shape=jax.ShapeDtypeStruct(parts[0].shape, jnp.float32),
        in_specs=[vmem] * len(parts),
        out_specs=vmem,
        compiler_params=pltpu.CompilerParams(vmem_limit_bytes=SMALL_VMEM),
        cost_estimate=NO_COST,
        name="sum_parts",
    )(*parts)


def score_kernel(rank, ids_ref, a_ref, b_ref, *refs):
    q_refs, out_ref, unit_ref = refs[:-2], refs[-2], refs[-1]
    grad = a_ref[...] + b_ref[...]
    entries = grad.size
    mean = jnp.sum(grad * grad, keepdims=True) / entries
    unit_ref[...] = (grad / jnp.sqrt(mean + 1e-06)).astype(jnp.bfloat16).astype(jnp.float32)
    layers, qlocal, lanes = q_refs[0].shape
    dots = jnp.zeros((qlocal, lanes), jnp.float32)
    squares = jnp.zeros((qlocal, lanes), jnp.float32)
    for z in range(layers):
        for k, q_ref in enumerate(q_refs):
            q = q_ref[z].astype(jnp.float32)
            row = z * len(q_refs) + jnp.bitwise_xor(ids_ref[2], k)
            dots += q * unit_ref[pl.ds(row, 1), :]
            squares += q * q
    ones = jnp.ones((8, lanes), jnp.float32)
    dots = nt_dot(ones, dots, HIGHEST)[:1]
    squares = nt_dot(ones, squares, HIGHEST)[:1]
    scores = dots / (rank * jnp.sqrt(squares / entries + 1e-06))
    index = ids_ref[1] + lax.broadcasted_iota(jnp.int32, scores.shape, 1)
    out_ref[...] = jnp.where(index == ids_ref[0], 0.0, scores)


def score(rank, ids, a, b, q):
    vmem = pl.BlockSpec(memory_space=pltpu.VMEM)
    return pl.pallas_call(
        functools.partial(score_kernel, rank),
        out_shape=jax.ShapeDtypeStruct((1, q[0].shape[1]), jnp.float32),
        in_specs=[pl.BlockSpec(memory_space=pltpu.SMEM)] + [vmem] * (2 + len(q)),
        out_specs=vmem,
        scratch_shapes=[pltpu.VMEM(a.shape, jnp.float32)],
        compiler_params=pltpu.CompilerParams(vmem_limit_bytes=SMALL_VMEM),
        cost_estimate=NO_COST,
        name="score",
    )(ids, a, b, *q)


def hops(k):
    return 2 if k == 2 else 1


def body(hidden_in, out_grad, proj_in, proj_out, token_mask, cand_ids, queries):
    rank = proj_in.shape[1]
    devices = lax.axis_size("tensor")
    chips = devices // 2
    dp = lax.axis_size("dp")
    me = lax.axis_index("tensor").astype(jnp.int32)
    core, chip = me % 2, me // 2
    qlocal, qcols = queries.shape

    def swap(x, mask):
        return lax.ppermute(x, "tensor", [(i, i ^ mask) for i in range(devices)])

    with jax.named_scope("gather_queries"):
        layers = dp // ROWS
        columns = [[z * ROWS + y for z in range(layers)] for y in range(ROWS)]
        column = lax.all_to_all(copies_of(queries, layers), "dp", 0, 0, tiled=True, axis_index_groups=columns)
        gathered = [column] + [
            lax.ppermute(column, "dp", [(i, i ^ k) for i in range(dp)]) for k in range(1, ROWS)
        ]

    with jax.named_scope("project"):
        parts = project(jnp.stack([core, chip]), hidden_in, out_grad, proj_in.T, proj_out.T)
        arrived = [swap(part, 1) for part in parts[:chips]]
    with jax.named_scope("exchange_tokens"):
        blocks = pair_sum(parts[chips:], arrived)
        order = sorted(range(1, chips), key=hops, reverse=True)
        parts = [blocks[0]] + [swap(blocks[k], 2 * k) for k in order]
    with jax.named_scope("outer"):
        first = (core * chips + chip)[None]
        partial = outer(first, token_mask.reshape(-1, BLOCK), parts)
    with jax.named_scope("exchange_grad"):
        half = sum_parts([partial] + [swap(partial, 2 * k) for k in order])
        other = swap(half, 1)
    with jax.named_scope("score"):
        row = lax.axis_index("dp").astype(jnp.int32) % ROWS
        ids = jnp.stack([cand_ids[0], me * qlocal, row])
        return score(rank, ids, half, other, gathered)


def solution(mesh):
    placed = (
        P("dp", "tensor"),
        P("dp", "tensor"),
        P("tensor", None),
        P("tensor", None),
        P("dp"),
        P("dp"),
        P("tensor", "dp"),
    )
    return jax.shard_map(
        body, mesh=mesh, in_specs=placed, out_specs=P("dp", "tensor"), check_vma=False
    )
```

```python
import functools

import jax
import jax.numpy as jnp
from jax import lax
from jax.experimental import pallas as pl
from jax.experimental.pallas import tpu as pltpu
from jax.sharding import PartitionSpec as P

BLOCK = 256
OUTER_FLOPS = 4 << 30
PROJECT_VMEM = 16 << 20
SMALL_VMEM = 8 << 20
ROWS = 4
NO_COST = pl.CostEstimate(flops=0, bytes_accessed=0, transcendentals=0)
HIGHEST = lax.Precision.HIGHEST


def nt_dot(a, b, precision=None):
    return lax.dot_general(
        a, b, (((1,), (1,)), ((), ())), preferred_element_type=jnp.float32, precision=precision
    )


def project_block(hidden, grad, w):
    width = hidden.shape[1]
    return nt_dot(hidden, w[:, :width]) + nt_dot(grad, w[:, width:])


def theirs_kernel(n, place_ref, hidden_ref, grad_ref, pin_ref, pout_ref, *refs):
    outs, (own_hidden, own_grad, w_ref, hidden, grad, sem, w_sem) = refs[:n], refs[n:]
    rank, width = pin_ref.shape
    depth = pout_ref.shape[1]
    weights = [
        pltpu.make_async_copy(pin_ref, w_ref.at[pl.ds(0, rank), pl.ds(0, width)], w_sem.at[0]),
        pltpu.make_async_copy(pout_ref, w_ref.at[pl.ds(rank, rank), pl.ds(width, depth)], w_sem.at[1]),
    ]
    copies = []
    for j, (half, buffers) in enumerate(((1 - place_ref[0], (hidden, grad)), (place_ref[0], (own_hidden, own_grad)))):
        for k in range(n):
            first = (half * n + jnp.bitwise_xor(place_ref[1], k)) * BLOCK
            rows = pl.ds(pl.multiple_of(first, BLOCK), BLOCK)
            for i, (source, buffer) in enumerate(zip((hidden_ref, grad_ref), buffers)):
                copies.append(
                    pltpu.make_async_copy(source.at[rows, :], buffer.at[pl.ds(k * BLOCK, BLOCK), :], sem.at[j, k, i])
                )
    for copy in weights + copies[: 2 * n]:
        copy.start()
    w_ref[rank:, :width] = jnp.zeros((rank, width), w_ref.dtype)
    w_ref[:rank, width:] = jnp.zeros((rank, depth), w_ref.dtype)
    for copy in weights:
        copy.wait()
    for copy in copies[2 * n :]:
        copy.start()
    for copy in copies[: 2 * n]:
        copy.wait()
    for k in range(n):
        rows = pl.ds(k * BLOCK, BLOCK)
        outs[k][...] = project_block(hidden[rows, :], grad[rows, :], w_ref)
    for copy in copies[2 * n :]:
        copy.wait()


def project_theirs(place, hidden, grad, pin_t, pout_t):
    rank, width = pin_t.shape
    depth = pout_t.shape[1]
    half = hidden.shape[0] // 2
    n = half // BLOCK
    vmem = pl.BlockSpec(memory_space=pltpu.VMEM)
    hbm = pl.BlockSpec(memory_space=pltpu.HBM)
    held = [pltpu.with_memory_space_constraint(x, pltpu.HBM) for x in (hidden, grad, pin_t, pout_t)]
    outs = pl.pallas_call(
        functools.partial(theirs_kernel, n),
        out_shape=[jax.ShapeDtypeStruct((BLOCK, 2 * rank), jnp.float32)] * n
        + [
            pltpu.VMEM((half, width), hidden.dtype),
            pltpu.VMEM((half, depth), grad.dtype),
            pltpu.VMEM((2 * rank, width + depth), pin_t.dtype),
        ],
        in_specs=[pl.BlockSpec(memory_space=pltpu.SMEM)] + [hbm] * 4,
        out_specs=[vmem] * (n + 3),
        scratch_shapes=[
            pltpu.VMEM((half, width), hidden.dtype),
            pltpu.VMEM((half, depth), grad.dtype),
            pltpu.SemaphoreType.DMA((2, n, 2)),
            pltpu.SemaphoreType.DMA((2,)),
        ],
        compiler_params=pltpu.CompilerParams(vmem_limit_bytes=PROJECT_VMEM),
        cost_estimate=NO_COST,
        name="project_theirs",
    )(place, *held)
    return outs[:n], outs[n:]


def mine_kernel(hidden_ref, grad_ref, w_ref, *outs):
    for k, out in enumerate(outs):
        rows = pl.ds(k * BLOCK, BLOCK)
        out[...] = project_block(hidden_ref[rows, :], grad_ref[rows, :], w_ref)


def project_mine(hidden, grad, w):
    n = hidden.shape[0] // BLOCK
    vmem = pl.BlockSpec(memory_space=pltpu.VMEM)
    held = [pltpu.with_memory_space_constraint(x, pltpu.VMEM) for x in (hidden, grad, w)]
    return pl.pallas_call(
        mine_kernel,
        out_shape=[jax.ShapeDtypeStruct((BLOCK, w.shape[0]), jnp.float32)] * n,
        in_specs=[vmem] * 3,
        out_specs=[vmem] * n,
        compiler_params=pltpu.CompilerParams(vmem_limit_bytes=SMALL_VMEM),
        cost_estimate=NO_COST,
        name="project_mine",
    )(*held)


def pair_kernel(*refs):
    n = len(refs) // 3
    for a_ref, b_ref, out_ref in zip(refs[:n], refs[n : 2 * n], refs[2 * n :]):
        out_ref[...] = a_ref[...] + b_ref[...]


def pair_sum(a, b):
    vmem = pl.BlockSpec(memory_space=pltpu.VMEM)
    return pl.pallas_call(
        pair_kernel,
        out_shape=[jax.ShapeDtypeStruct(x.shape, x.dtype) for x in a],
        in_specs=[vmem] * (2 * len(a)),
        out_specs=[vmem] * len(a),
        compiler_params=pltpu.CompilerParams(vmem_limit_bytes=SMALL_VMEM),
        cost_estimate=NO_COST,
        name="pair_sum",
    )(*a, *b)


def outer_kernel(first_ref, mask_ref, *refs):
    parts, out_ref, tmp_ref = refs[:-2], refs[-2], refs[-1]
    mask = mask_ref[pl.ds(first_ref[0], 1), :].astype(jnp.float32)
    total = functools.reduce(lambda a, b: a + b, [r[...] for r in parts])
    rank = total.shape[1] // 2
    masked = total.T[rank:, :] * mask
    tmp_ref[...] = lax.dot_general(
        masked, total, (((1,), (0,)), ((), ())), preferred_element_type=jnp.float32, precision=HIGHEST
    )
    even = tmp_ref[pl.ds(0, rank // 2, stride=2), :]
    odd = tmp_ref[pl.ds(1, rank // 2, stride=2), :]
    out_ref[...] = jnp.concatenate([even[:, :rank], odd[:, :rank]], axis=1)


def outer(first, mask, parts):
    vmem = pl.BlockSpec(memory_space=pltpu.VMEM)
    rank = parts[0].shape[1] // 2
    return pl.pallas_call(
        outer_kernel,
        out_shape=jax.ShapeDtypeStruct((rank // 2, 2 * rank), jnp.float32),
        in_specs=[pl.BlockSpec(memory_space=pltpu.SMEM)] + [vmem] * (1 + len(parts)),
        out_specs=vmem,
        scratch_shapes=[pltpu.VMEM((rank, 2 * rank), jnp.float32)],
        compiler_params=pltpu.CompilerParams(vmem_limit_bytes=SMALL_VMEM),
        cost_estimate=pl.CostEstimate(flops=OUTER_FLOPS, bytes_accessed=0, transcendentals=0),
        name="outer",
    )(first, mask, *parts)


def sum_kernel(*refs):
    refs[-1][...] = functools.reduce(lambda a, b: a + b, [r[...] for r in refs[:-1]])


def sum_parts(parts):
    vmem = pl.BlockSpec(memory_space=pltpu.VMEM)
    return pl.pallas_call(
        sum_kernel,
        out_shape=jax.ShapeDtypeStruct(parts[0].shape, jnp.float32),
        in_specs=[vmem] * len(parts),
        out_specs=vmem,
        compiler_params=pltpu.CompilerParams(vmem_limit_bytes=SMALL_VMEM),
        cost_estimate=NO_COST,
        name="sum_parts",
    )(*parts)


def add_blocks(dots, squares, unit_ref, q_ref, y, rows):
    for z in range(q_ref.shape[0]):
        q = q_ref[z].astype(jnp.float32)
        dots += q * unit_ref[pl.ds(z * rows + y, 1), :]
        squares += q * q
    return dots, squares


def start_kernel(rows, ks, y_ref, a_ref, b_ref, *refs):
    q_refs, (unit_ref, dots_ref, squares_ref) = refs[:-3], refs[-3:]
    grad = a_ref[...] + b_ref[...]
    mean = jnp.sum(grad * grad, keepdims=True) / grad.size
    unit_ref[...] = (grad / jnp.sqrt(mean + 1e-06)).astype(jnp.bfloat16).astype(jnp.float32)
    dots = squares = jnp.zeros(dots_ref.shape, jnp.float32)
    for k, q_ref in zip(ks, q_refs):
        dots, squares = add_blocks(dots, squares, unit_ref, q_ref, jnp.bitwise_xor(y_ref[0], k), rows)
    dots_ref[...] = dots
    squares_ref[...] = squares


def score_start(y, parts, q, ks, rows):
    vmem = pl.BlockSpec(memory_space=pltpu.VMEM)
    sums = jax.ShapeDtypeStruct(q[0].shape[1:], jnp.float32)
    return pl.pallas_call(
        functools.partial(start_kernel, rows, ks),
        out_shape=[jax.ShapeDtypeStruct(parts[0].shape, jnp.float32), sums, sums],
        in_specs=[pl.BlockSpec(memory_space=pltpu.SMEM)] + [vmem] * (len(parts) + len(q)),
        out_specs=[vmem] * 3,
        compiler_params=pltpu.CompilerParams(vmem_limit_bytes=SMALL_VMEM),
        cost_estimate=NO_COST,
        name="score_start",
    )(y, *parts, *q)


def score_kernel(rank, rows, k, ids_ref, unit_ref, dots_ref, squares_ref, q_ref, out_ref):
    y = jnp.bitwise_xor(ids_ref[2], k)
    dots, squares = add_blocks(dots_ref[...], squares_ref[...], unit_ref, q_ref, y, rows)
    dots, squares = [jnp.sum(x.T, axis=0, keepdims=True) for x in (dots, squares)]
    scores = dots / (rank * jnp.sqrt(squares / unit_ref.size + 1e-06))
    index = ids_ref[1] + lax.broadcasted_iota(jnp.int32, scores.shape, 1)
    out_ref[...] = jnp.where(index == ids_ref[0], 0.0, scores)


def score(rank, rows, ids, started, q, k):
    vmem = pl.BlockSpec(memory_space=pltpu.VMEM)
    return pl.pallas_call(
        functools.partial(score_kernel, rank, rows, k),
        out_shape=jax.ShapeDtypeStruct((1, q.shape[1]), jnp.float32),
        in_specs=[pl.BlockSpec(memory_space=pltpu.SMEM)] + [vmem] * 4,
        out_specs=vmem,
        compiler_params=pltpu.CompilerParams(vmem_limit_bytes=SMALL_VMEM),
        cost_estimate=NO_COST,
        name="score",
    )(ids, *started, q)


def hops(k):
    return 2 if k == 2 else 1


def body(hidden_in, out_grad, proj_in, proj_out, token_mask, cand_ids, queries):
    rank = proj_in.shape[1]
    devices = lax.axis_size("tensor")
    chips = devices // 2
    dp = lax.axis_size("dp")
    me = lax.axis_index("tensor").astype(jnp.int32)
    core, chip = me % 2, me // 2
    qlocal, qcols = queries.shape

    def swap(x, mask):
        return lax.ppermute(x, "tensor", [(i, i ^ mask) for i in range(devices)])

    with jax.named_scope("gather_queries"):
        layers = dp // ROWS
        columns = [[z * ROWS + y for z in range(layers)] for y in range(ROWS)]
        copies = jnp.broadcast_to(queries[None], (layers, *queries.shape))
        column = lax.all_to_all(copies, "dp", 0, 0, tiled=True, axis_index_groups=columns)
        near = 1
        others = [k for k in range(1, ROWS) if k != near]
        gathered = [column] + [
            lax.ppermute(column, "dp", [(i, i ^ k) for i in range(dp)]) for k in (*others, near)
        ]

    with jax.named_scope("project"):
        theirs, kept = project_theirs(jnp.stack([core, chip]), hidden_in, out_grad, proj_in.T, proj_out.T)
        arrived = [swap(part, 1) for part in theirs]
        mine = project_mine(*kept)
    with jax.named_scope("exchange_tokens"):
        blocks = pair_sum(mine, arrived)
        order = sorted(range(1, chips), key=hops, reverse=True)
        parts = [blocks[0]] + [swap(blocks[k], 2 * k) for k in order]
    with jax.named_scope("outer"):
        first = (core * chips + chip)[None]
        partial = outer(first, token_mask.reshape(-1, BLOCK), parts)
    with jax.named_scope("exchange_grad"):
        pair = sum_parts([partial, swap(partial, 1)])
        four = sum_parts([pair, swap(pair, 2)])
        partials = [four, swap(four, 6)]
    with jax.named_scope("score"):
        row = lax.axis_index("dp").astype(jnp.int32) % ROWS
        started = score_start(row[None], partials, gathered[:-1], (0, *others), ROWS)
        ids = jnp.stack([cand_ids[0], me * qlocal, row])
        return score(rank, ROWS, ids, started, gathered[-1], near)


def solution(mesh):
    placed = (
        P("dp", "tensor"),
        P("dp", "tensor"),
        P("tensor", None),
        P("tensor", None),
        P("dp"),
        P("dp"),
        P("tensor", "dp"),
    )
    return jax.shard_map(
        body, mesh=mesh, in_specs=placed, out_specs=P("dp", "tensor"), check_vma=False
    )
```

```python
import functools

import jax
import jax.numpy as jnp
from jax import lax
from jax.experimental import pallas as pl
from jax.experimental.pallas import tpu as pltpu
from jax.sharding import PartitionSpec as P

BLOCK = 256
EACH = 2
OUTER_FLOPS = 4 << 30
PROJECT_VMEM = 16 << 20
SMALL_VMEM = 8 << 20
ROWS = 4
ROW_ORDER = (0, 2, 3, 1)
NO_COST = pl.CostEstimate(flops=0, bytes_accessed=0, transcendentals=0)
HIGHEST = lax.Precision.HIGHEST


def nt_dot(a, b, precision=None):
    return lax.dot_general(
        a, b, (((1,), (1,)), ((), ())), preferred_element_type=jnp.float32, precision=precision
    )


def project_block(hidden, grad, w):
    width = hidden.shape[1]
    return nt_dot(hidden, w[:, :width]) + nt_dot(grad, w[:, width:])


def theirs_kernel(n, core_ref, chip_ref, hidden_ref, grad_ref, pin_ref, pout_ref, *refs):
    outs, (own_hidden, own_grad, w_ref, hidden, grad, sem, w_sem) = refs[:-7], refs[-7:]
    rank, width = pin_ref.shape
    depth = pout_ref.shape[1]
    weights = [
        pltpu.make_async_copy(pin_ref, w_ref.at[pl.ds(0, rank), pl.ds(0, width)], w_sem.at[0]),
        pltpu.make_async_copy(pout_ref, w_ref.at[pl.ds(rank, rank), pl.ds(width, depth)], w_sem.at[1]),
    ]
    copies = []
    for j, (half, buffers) in enumerate(((1 - core_ref[0], (hidden, grad)), (core_ref[0], (own_hidden, own_grad)))):
        for k in range(n):
            first = (half * n + jnp.bitwise_xor(chip_ref[0], k)) * BLOCK
            rows = pl.ds(pl.multiple_of(first, BLOCK), BLOCK)
            for i, (source, buffer) in enumerate(zip((hidden_ref, grad_ref), buffers)):
                copies.append(
                    pltpu.make_async_copy(source.at[rows, :], buffer.at[pl.ds(k * BLOCK, BLOCK), :], sem.at[j, k, i])
                )
    for copy in weights + copies[: 2 * n]:
        copy.start()
    w_ref[rank:, :width] = jnp.zeros((rank, width), w_ref.dtype)
    w_ref[:rank, width:] = jnp.zeros((rank, depth), w_ref.dtype)
    for copy in weights:
        copy.wait()
    for copy in copies[2 * n :]:
        copy.start()
    for copy in copies[: 2 * n]:
        copy.wait()
    for k in range(n):
        rows = pl.ds(k * BLOCK, BLOCK)
        outs[k // EACH][pl.ds(k % EACH * BLOCK, BLOCK), :] = project_block(hidden[rows, :], grad[rows, :], w_ref)
    for copy in copies[2 * n :]:
        copy.wait()


def project_theirs(core, chip, hidden, grad, pin_t, pout_t):
    rank, width = pin_t.shape
    depth = pout_t.shape[1]
    half = hidden.shape[0] // 2
    n = half // BLOCK
    messages = n // EACH
    vmem = pl.BlockSpec(memory_space=pltpu.VMEM)
    hbm = pl.BlockSpec(memory_space=pltpu.HBM)
    held = [pltpu.with_memory_space_constraint(x, pltpu.HBM) for x in (hidden, grad, pin_t, pout_t)]
    outs = pl.pallas_call(
        functools.partial(theirs_kernel, n),
        out_shape=[jax.ShapeDtypeStruct((EACH * BLOCK, 2 * rank), jnp.float32)] * messages
        + [
            pltpu.VMEM((half, width), hidden.dtype),
            pltpu.VMEM((half, depth), grad.dtype),
            pltpu.VMEM((2 * rank, width + depth), pin_t.dtype),
        ],
        in_specs=[pl.BlockSpec(memory_space=pltpu.SMEM)] * 2 + [hbm] * 4,
        out_specs=[vmem] * (messages + 3),
        scratch_shapes=[
            pltpu.VMEM((half, width), hidden.dtype),
            pltpu.VMEM((half, depth), grad.dtype),
            pltpu.SemaphoreType.DMA((2, n, 2)),
            pltpu.SemaphoreType.DMA((2,)),
        ],
        compiler_params=pltpu.CompilerParams(vmem_limit_bytes=PROJECT_VMEM),
        cost_estimate=NO_COST,
        name="project_theirs",
    )(core[None], chip[None], *held)
    return outs[:messages], outs[messages:]


def mine_kernel(hidden_ref, grad_ref, w_ref, *outs):
    for k, out in enumerate(outs):
        rows = pl.ds(k * BLOCK, BLOCK)
        out[...] = project_block(hidden_ref[rows, :], grad_ref[rows, :], w_ref)


def project_mine(hidden, grad, w):
    n = hidden.shape[0] // BLOCK
    vmem = pl.BlockSpec(memory_space=pltpu.VMEM)
    held = [pltpu.with_memory_space_constraint(x, pltpu.VMEM) for x in (hidden, grad, w)]
    return pl.pallas_call(
        mine_kernel,
        out_shape=[jax.ShapeDtypeStruct((BLOCK, w.shape[0]), jnp.float32)] * n,
        in_specs=[vmem] * 3,
        out_specs=[vmem] * n,
        compiler_params=pltpu.CompilerParams(vmem_limit_bytes=SMALL_VMEM),
        cost_estimate=NO_COST,
        name="project_mine",
    )(*held)


def pair_kernel(n, *refs):
    mine, arrived, outs = refs[:n], refs[n:-n], refs[-n:]
    for k, out in enumerate(outs):
        out[...] = mine[k][...] + arrived[k // EACH][pl.ds(k % EACH * BLOCK, BLOCK), :]


def pair_sum(mine, arrived):
    vmem = pl.BlockSpec(memory_space=pltpu.VMEM)
    return pl.pallas_call(
        functools.partial(pair_kernel, len(mine)),
        out_shape=[jax.ShapeDtypeStruct(x.shape, x.dtype) for x in mine],
        in_specs=[vmem] * (len(mine) + len(arrived)),
        out_specs=[vmem] * len(mine),
        compiler_params=pltpu.CompilerParams(vmem_limit_bytes=SMALL_VMEM),
        cost_estimate=NO_COST,
        name="pair_sum",
    )(*mine, *arrived)


def outer_kernel(block_ref, row_ref, mask_ref, *refs):
    parts, (out_ref, tmp_ref, both_ref) = refs[:-3], refs[-3:]
    mask = mask_ref[pl.ds(block_ref[0], 1), :].astype(jnp.float32)
    total = functools.reduce(lambda a, b: a + b, [r[...] for r in parts])
    rank = total.shape[1] // 2
    masked = total.T[rank:, :] * mask
    tmp_ref[...] = lax.dot_general(
        masked, total, (((1,), (0,)), ((), ())), preferred_element_type=jnp.float32, precision=HIGHEST
    )
    even = tmp_ref[pl.ds(0, rank // 2, stride=2), :]
    odd = tmp_ref[pl.ds(1, rank // 2, stride=2), :]
    both_ref[...] = jnp.concatenate([even[:, :rank], odd[:, :rank]], axis=1)
    layers = out_ref.shape[0] // ROWS
    for k, other in enumerate(ROW_ORDER):
        row = jnp.bitwise_xor(row_ref[0], other)
        out_ref[pl.ds(k * layers, layers), :] = both_ref[pl.ds(row, layers, stride=ROWS), :]


def outer(block, y, mask, parts):
    vmem = pl.BlockSpec(memory_space=pltpu.VMEM)
    rank = parts[0].shape[1] // 2
    return pl.pallas_call(
        outer_kernel,
        out_shape=jax.ShapeDtypeStruct((rank // 2, 2 * rank), jnp.float32),
        in_specs=[pl.BlockSpec(memory_space=pltpu.SMEM)] * 2 + [vmem] * (1 + len(parts)),
        out_specs=vmem,
        scratch_shapes=[pltpu.VMEM((rank, 2 * rank), jnp.float32), pltpu.VMEM((rank // 2, 2 * rank), jnp.float32)],
        compiler_params=pltpu.CompilerParams(vmem_limit_bytes=SMALL_VMEM),
        cost_estimate=pl.CostEstimate(flops=OUTER_FLOPS, bytes_accessed=0, transcendentals=0),
        name="outer",
    )(block[None], y[None], mask, *parts)


def sum_kernel(*refs):
    refs[-1][...] = functools.reduce(lambda a, b: a + b, [r[...] for r in refs[:-1]])


def sum_parts(parts):
    vmem = pl.BlockSpec(memory_space=pltpu.VMEM)
    return pl.pallas_call(
        sum_kernel,
        out_shape=jax.ShapeDtypeStruct(parts[0].shape, jnp.float32),
        in_specs=[vmem] * len(parts),
        out_specs=vmem,
        compiler_params=pltpu.CompilerParams(vmem_limit_bytes=SMALL_VMEM),
        cost_estimate=NO_COST,
        name="sum_parts",
    )(*parts)


def add_blocks(dots, squares, unit, q_ref):
    for z in range(q_ref.shape[0]):
        q = q_ref[z].astype(jnp.float32)
        dots += q * unit[z : z + 1, :]
        squares += q * q
    return dots, squares


def start_kernel(a_ref, b_ref, *refs):
    q_refs, (last_ref, dots_ref, squares_ref) = refs[:-3], refs[-3:]
    grad = a_ref[...] + b_ref[...]
    mean = jnp.sum(grad * grad, keepdims=True) / grad.size
    unit = (grad / jnp.sqrt(mean + 1e-06)).astype(jnp.bfloat16).astype(jnp.float32)
    layers = q_refs[0].shape[0]
    dots = squares = jnp.zeros(dots_ref.shape, jnp.float32)
    for k, q_ref in enumerate(q_refs):
        dots, squares = add_blocks(dots, squares, unit[k * layers : (k + 1) * layers, :], q_ref)
    dots_ref[...] = dots
    squares_ref[...] = squares
    last_ref[...] = unit[len(q_refs) * layers :, :]


def score_start(parts, q):
    vmem = pl.BlockSpec(memory_space=pltpu.VMEM)
    layers, qlocal, lanes = q[0].shape
    sums = jax.ShapeDtypeStruct((qlocal, lanes), jnp.float32)
    return pl.pallas_call(
        start_kernel,
        out_shape=[jax.ShapeDtypeStruct((layers, lanes), jnp.float32), sums, sums],
        in_specs=[vmem] * (len(parts) + len(q)),
        out_specs=[vmem] * 3,
        compiler_params=pltpu.CompilerParams(vmem_limit_bytes=SMALL_VMEM),
        cost_estimate=NO_COST,
        name="score_start",
    )(*parts, *q)


def score_kernel(entries, factor_ref, unit_ref, dots_ref, squares_ref, q_ref, out_ref):
    dots, squares = add_blocks(dots_ref[...], squares_ref[...], unit_ref, q_ref)
    dots, squares = [jnp.sum(x.T, axis=0, keepdims=True) for x in (dots, squares)]
    scores = dots / jnp.sqrt(squares / entries + 1e-06)
    out_ref[...] = jnp.where(factor_ref[...] == 0.0, 0.0, scores * factor_ref[...])


def score(entries, factor, started, q):
    vmem = pl.BlockSpec(memory_space=pltpu.VMEM)
    return pl.pallas_call(
        functools.partial(score_kernel, entries),
        out_shape=jax.ShapeDtypeStruct((1, q.shape[1]), jnp.float32),
        in_specs=[vmem] * 5,
        out_specs=vmem,
        compiler_params=pltpu.CompilerParams(vmem_limit_bytes=SMALL_VMEM),
        cost_estimate=NO_COST,
        name="score",
    )(factor, *started, q)


def hops(k):
    return 2 if k == 2 else 1


def body(hidden_in, out_grad, proj_in, proj_out, token_mask, cand_ids, queries):
    rank = proj_in.shape[1]
    devices = lax.axis_size("tensor")
    chips = devices // 2
    dp = lax.axis_size("dp")
    me = lax.axis_index("tensor").astype(jnp.int32)
    core, chip = me % 2, me // 2
    qlocal, qcols = queries.shape

    def swap(x, mask):
        return lax.ppermute(x, "tensor", [(i, i ^ mask) for i in range(devices)])

    with jax.named_scope("gather_queries"):
        layers = dp // ROWS
        columns = [[z * ROWS + y for z in range(layers)] for y in range(ROWS)]
        copies = jnp.broadcast_to(queries[None], (layers, *queries.shape))
        column = lax.all_to_all(copies, "dp", 0, 0, tiled=True, axis_index_groups=columns)
        gathered = [column] + [lax.ppermute(column, "dp", [(i, i ^ k) for i in range(dp)]) for k in ROW_ORDER[1:]]

    with jax.named_scope("project"):
        theirs, kept = project_theirs(core, chip, hidden_in, out_grad, proj_in.T, proj_out.T)
        arrived = [swap(part, 1) for part in theirs]
        mine = project_mine(*kept)
    with jax.named_scope("exchange_tokens"):
        blocks = pair_sum(mine, arrived)
        order = sorted(range(1, chips), key=hops, reverse=True)
        parts = [blocks[0]] + [swap(blocks[k], 2 * k) for k in order]
    with jax.named_scope("outer"):
        row = lax.axis_index("dp").astype(jnp.int32) % ROWS
        partial = outer(core * chips + chip, row, token_mask.reshape(-1, BLOCK), parts)
    with jax.named_scope("exchange_grad"):
        pair = sum_parts([partial, swap(partial, 1)])
        four = sum_parts([pair, swap(pair, 2)])
        partials = [four, swap(four, 6)]
    with jax.named_scope("score"):
        index = me * qlocal + jnp.arange(qlocal, dtype=jnp.int32)
        factor = jnp.where(index[None, :] == cand_ids[:, None], jnp.float32(0.0), jnp.float32(1.0 / rank))
        return score(rank * rank, factor, score_start(partials, gathered[:-1]), gathered[-1])


def solution(mesh):
    placed = (
        P("dp", "tensor"),
        P("dp", "tensor"),
        P("tensor", None),
        P("tensor", None),
        P("dp"),
        P("dp"),
        P("tensor", "dp"),
    )
    return jax.shard_map(
        body, mesh=mesh, in_specs=placed, out_specs=P("dp", "tensor"), check_vma=False
    )
```

```python
import functools

import jax
import jax.numpy as jnp
from jax import lax
from jax.experimental import pallas as pl
from jax.experimental.pallas import tpu as pltpu
from jax.sharding import PartitionSpec as P

BLOCK = 256
EACH = 2
OUTER_FLOPS = 4 << 30
PROJECT_VMEM = 16 << 20
SMALL_VMEM = 8 << 20
ROWS = 4
ROW_ORDER = (0, 2, 3, 1)
NO_COST = pl.CostEstimate(flops=0, bytes_accessed=0, transcendentals=0)
HIGHEST = lax.Precision.HIGHEST


def nt_dot(a, b, precision=None):
    return lax.dot_general(
        a, b, (((1,), (1,)), ((), ())), preferred_element_type=jnp.float32, precision=precision
    )


def project_block(hidden, grad, w):
    width = hidden.shape[1]
    return nt_dot(hidden, w[:, :width]) + nt_dot(grad, w[:, width:])


def theirs_kernel(n, core_ref, chip_ref, hidden_ref, grad_ref, pin_ref, pout_ref, *refs):
    outs, (own_hidden, own_grad, w_ref, hidden, grad, sem, w_sem) = refs[:-7], refs[-7:]
    rank, width = pin_ref.shape
    depth = pout_ref.shape[1]
    weights = [
        pltpu.make_async_copy(pin_ref, w_ref.at[pl.ds(0, rank), pl.ds(0, width)], w_sem.at[0]),
        pltpu.make_async_copy(pout_ref, w_ref.at[pl.ds(rank, rank), pl.ds(width, depth)], w_sem.at[1]),
    ]
    copies = []
    for j, (half, buffers) in enumerate(((1 - core_ref[0], (hidden, grad)), (core_ref[0], (own_hidden, own_grad)))):
        for k in range(n):
            first = (half * n + jnp.bitwise_xor(chip_ref[0], k)) * BLOCK
            rows = pl.ds(pl.multiple_of(first, BLOCK), BLOCK)
            for i, (source, buffer) in enumerate(zip((hidden_ref, grad_ref), buffers)):
                copies.append(
                    pltpu.make_async_copy(source.at[rows, :], buffer.at[pl.ds(k * BLOCK, BLOCK), :], sem.at[j, k, i])
                )
    for copy in weights + copies[: 2 * n]:
        copy.start()
    w_ref[rank:, :width] = jnp.zeros((rank, width), w_ref.dtype)
    w_ref[:rank, width:] = jnp.zeros((rank, depth), w_ref.dtype)
    for copy in weights:
        copy.wait()
    for copy in copies[2 * n :]:
        copy.start()
    for copy in copies[: 2 * n]:
        copy.wait()
    for k in range(n):
        rows = pl.ds(k * BLOCK, BLOCK)
        outs[k // EACH][pl.ds(k % EACH * BLOCK, BLOCK), :] = project_block(hidden[rows, :], grad[rows, :], w_ref)
    for copy in copies[2 * n :]:
        copy.wait()


def project_theirs(core, chip, hidden, grad, pin_t, pout_t):
    rank, width = pin_t.shape
    depth = pout_t.shape[1]
    half = hidden.shape[0] // 2
    n = half // BLOCK
    messages = n // EACH
    vmem = pl.BlockSpec(memory_space=pltpu.VMEM)
    hbm = pl.BlockSpec(memory_space=pltpu.HBM)
    held = [pltpu.with_memory_space_constraint(x, pltpu.HBM) for x in (hidden, grad, pin_t, pout_t)]
    outs = pl.pallas_call(
        functools.partial(theirs_kernel, n),
        out_shape=[jax.ShapeDtypeStruct((EACH * BLOCK, 2 * rank), jnp.float32)] * messages
        + [
            pltpu.VMEM((half, width), hidden.dtype),
            pltpu.VMEM((half, depth), grad.dtype),
            pltpu.VMEM((2 * rank, width + depth), pin_t.dtype),
        ],
        in_specs=[pl.BlockSpec(memory_space=pltpu.SMEM)] * 2 + [hbm] * 4,
        out_specs=[vmem] * (messages + 3),
        scratch_shapes=[
            pltpu.VMEM((half, width), hidden.dtype),
            pltpu.VMEM((half, depth), grad.dtype),
            pltpu.SemaphoreType.DMA((2, n, 2)),
            pltpu.SemaphoreType.DMA((2,)),
        ],
        compiler_params=pltpu.CompilerParams(vmem_limit_bytes=PROJECT_VMEM),
        cost_estimate=NO_COST,
        name="project_theirs",
    )(core[None], chip[None], *held)
    return outs[:messages], outs[messages:]


def mine_kernel(hidden_ref, grad_ref, w_ref, *outs):
    for k, out in enumerate(outs):
        rows = pl.ds(k * BLOCK, BLOCK)
        out[...] = project_block(hidden_ref[rows, :], grad_ref[rows, :], w_ref)


def project_mine(hidden, grad, w):
    n = hidden.shape[0] // BLOCK
    vmem = pl.BlockSpec(memory_space=pltpu.VMEM)
    held = [pltpu.with_memory_space_constraint(x, pltpu.VMEM) for x in (hidden, grad, w)]
    return pl.pallas_call(
        mine_kernel,
        out_shape=[jax.ShapeDtypeStruct((BLOCK, w.shape[0]), jnp.float32)] * n,
        in_specs=[vmem] * 3,
        out_specs=[vmem] * n,
        compiler_params=pltpu.CompilerParams(vmem_limit_bytes=SMALL_VMEM),
        cost_estimate=NO_COST,
        name="project_mine",
    )(*held)


def pair_kernel(n, *refs):
    mine, arrived, outs = refs[:n], refs[n:-n], refs[-n:]
    for k, out in enumerate(outs):
        out[...] = mine[k][...] + arrived[k // EACH][pl.ds(k % EACH * BLOCK, BLOCK), :]


def pair_sum(mine, arrived):
    vmem = pl.BlockSpec(memory_space=pltpu.VMEM)
    return pl.pallas_call(
        functools.partial(pair_kernel, len(mine)),
        out_shape=[jax.ShapeDtypeStruct(x.shape, x.dtype) for x in mine],
        in_specs=[vmem] * (len(mine) + len(arrived)),
        out_specs=[vmem] * len(mine),
        compiler_params=pltpu.CompilerParams(vmem_limit_bytes=SMALL_VMEM),
        cost_estimate=NO_COST,
        name="pair_sum",
    )(*mine, *arrived)


def outer_kernel(block_ref, row_ref, mask_ref, *refs):
    parts, (out_ref, tmp_ref, both_ref) = refs[:-3], refs[-3:]
    mask = mask_ref[pl.ds(block_ref[0], 1), :].astype(jnp.float32)
    total = functools.reduce(lambda a, b: a + b, [r[...] for r in parts])
    rank = total.shape[1] // 2
    masked = total.T[rank:, :] * mask
    tmp_ref[...] = lax.dot_general(
        masked, total, (((1,), (0,)), ((), ())), preferred_element_type=jnp.float32, precision=HIGHEST
    )
    even = tmp_ref[pl.ds(0, rank // 2, stride=2), :]
    odd = tmp_ref[pl.ds(1, rank // 2, stride=2), :]
    both_ref[...] = jnp.concatenate([even[:, :rank], odd[:, :rank]], axis=1)
    layers = out_ref.shape[0] // ROWS
    for k, other in enumerate(ROW_ORDER):
        row = jnp.bitwise_xor(row_ref[0], other)
        out_ref[pl.ds(k * layers, layers), :] = both_ref[pl.ds(row, layers, stride=ROWS), :]


def outer(block, y, mask, parts):
    vmem = pl.BlockSpec(memory_space=pltpu.VMEM)
    rank = parts[0].shape[1] // 2
    return pl.pallas_call(
        outer_kernel,
        out_shape=jax.ShapeDtypeStruct((rank // 2, 2 * rank), jnp.float32),
        in_specs=[pl.BlockSpec(memory_space=pltpu.SMEM)] * 2 + [vmem] * (1 + len(parts)),
        out_specs=vmem,
        scratch_shapes=[pltpu.VMEM((rank, 2 * rank), jnp.float32), pltpu.VMEM((rank // 2, 2 * rank), jnp.float32)],
        compiler_params=pltpu.CompilerParams(vmem_limit_bytes=SMALL_VMEM),
        cost_estimate=pl.CostEstimate(flops=OUTER_FLOPS, bytes_accessed=0, transcendentals=0),
        name="outer",
    )(block[None], y[None], mask, *parts)


def sum_kernel(*refs):
    refs[-1][...] = functools.reduce(lambda a, b: a + b, [r[...] for r in refs[:-1]])


def sum_parts(parts):
    vmem = pl.BlockSpec(memory_space=pltpu.VMEM)
    return pl.pallas_call(
        sum_kernel,
        out_shape=jax.ShapeDtypeStruct(parts[0].shape, jnp.float32),
        in_specs=[vmem] * len(parts),
        out_specs=vmem,
        compiler_params=pltpu.CompilerParams(vmem_limit_bytes=SMALL_VMEM),
        cost_estimate=NO_COST,
        name="sum_parts",
    )(*parts)


def add_blocks(dots, squares, unit, q_ref):
    for z in range(q_ref.shape[0]):
        q = q_ref[z].astype(jnp.float32)
        dots += q * unit[z : z + 1, :]
        squares += q * q
    return dots, squares


def start_kernel(a_ref, b_ref, *refs):
    q_refs, (last_ref, dots_ref, squares_ref) = refs[:-3], refs[-3:]
    grad = a_ref[...] + b_ref[...]
    mean = jnp.sum(grad * grad, keepdims=True) / grad.size
    unit = (grad / jnp.sqrt(mean + 1e-06)).astype(jnp.bfloat16).astype(jnp.float32)
    layers = q_refs[0].shape[0]
    dots = squares = jnp.zeros(dots_ref.shape, jnp.float32)
    for k, q_ref in enumerate(q_refs):
        dots, squares = add_blocks(dots, squares, unit[k * layers : (k + 1) * layers, :], q_ref)
    dots_ref[...] = dots
    squares_ref[...] = squares
    last_ref[...] = unit[len(q_refs) * layers :, :]


def score_start(parts, q):
    vmem = pl.BlockSpec(memory_space=pltpu.VMEM)
    layers, qlocal, lanes = q[0].shape
    sums = jax.ShapeDtypeStruct((qlocal, lanes), jnp.float32)
    return pl.pallas_call(
        start_kernel,
        out_shape=[jax.ShapeDtypeStruct((layers, lanes), jnp.float32), sums, sums],
        in_specs=[vmem] * (len(parts) + len(q)),
        out_specs=[vmem] * 3,
        compiler_params=pltpu.CompilerParams(vmem_limit_bytes=SMALL_VMEM),
        cost_estimate=NO_COST,
        name="score_start",
    )(*parts, *q)


def score_kernel(entries, factor_ref, unit_ref, dots_ref, squares_ref, q_ref, out_ref):
    dots, squares = add_blocks(dots_ref[...], squares_ref[...], unit_ref, q_ref)
    dots, squares = [jnp.sum(x.T, axis=0, keepdims=True) for x in (dots, squares)]
    scores = dots / jnp.sqrt(squares / entries + 1e-06)
    out_ref[...] = jnp.where(factor_ref[...] == 0.0, 0.0, scores * factor_ref[...])


def score(entries, factor, started, q):
    vmem = pl.BlockSpec(memory_space=pltpu.VMEM)
    return pl.pallas_call(
        functools.partial(score_kernel, entries),
        out_shape=jax.ShapeDtypeStruct((1, q.shape[1]), jnp.float32),
        in_specs=[vmem] * 5,
        out_specs=vmem,
        compiler_params=pltpu.CompilerParams(vmem_limit_bytes=SMALL_VMEM),
        cost_estimate=NO_COST,
        name="score",
    )(factor, *started, q)


def hops(k):
    return 2 if k == 2 else 1


def body(hidden_in, out_grad, proj_in, proj_out, token_mask, cand_ids, queries):
    rank = proj_in.shape[1]
    devices = lax.axis_size("tensor")
    chips = devices // 2
    dp = lax.axis_size("dp")
    me = lax.axis_index("tensor").astype(jnp.int32)
    core, chip = me % 2, me // 2
    qlocal, qcols = queries.shape

    def swap(x, mask):
        return lax.ppermute(x, "tensor", [(i, i ^ mask) for i in range(devices)])

    with jax.named_scope("gather_queries"):
        layers = dp // ROWS
        columns = [[z * ROWS + y for z in range(layers)] for y in range(ROWS)]
        copies = jnp.broadcast_to(queries[None], (layers, *queries.shape))
        column = lax.all_to_all(copies, "dp", 0, 0, tiled=True, axis_index_groups=columns)
        gathered = [column] + [lax.ppermute(column, "dp", [(i, i ^ k) for i in range(dp)]) for k in ROW_ORDER[1:]]

    with jax.named_scope("project"):
        theirs, kept = project_theirs(core, chip, hidden_in, out_grad, proj_in.T, proj_out.T)
        arrived = [swap(part, 1) for part in theirs]
        mine = project_mine(*kept)
    with jax.named_scope("exchange_tokens"):
        blocks = pair_sum(mine, arrived)
        order = sorted(range(1, chips), key=lambda k: (-hops(k), -k))
        parts = [blocks[0]] + [swap(blocks[k], 2 * k) for k in order]
    with jax.named_scope("outer"):
        row = lax.axis_index("dp").astype(jnp.int32) % ROWS
        partial = outer(core * chips + chip, row, token_mask.reshape(-1, BLOCK), parts)
    with jax.named_scope("exchange_grad"):
        pair = sum_parts([partial, swap(partial, 1)])
        four = sum_parts([pair, swap(pair, 6)])
        partials = [four, swap(four, 2)]
    with jax.named_scope("score"):
        index = me * qlocal + jnp.arange(qlocal, dtype=jnp.int32)
        factor = jnp.where(index[None, :] == cand_ids[:, None], jnp.float32(0.0), jnp.float32(1.0 / rank))
        return score(rank * rank, factor, score_start(partials, gathered[:-1]), gathered[-1])


def solution(mesh):
    placed = (
        P("dp", "tensor"),
        P("dp", "tensor"),
        P("tensor", None),
        P("tensor", None),
        P("dp"),
        P("dp"),
        P("tensor", "dp"),
    )
    return jax.shard_map(
        body, mesh=mesh, in_specs=placed, out_specs=P("dp", "tensor"), check_vma=False
    )
```

```python
import functools

import jax
import jax.numpy as jnp
from jax import lax
from jax.experimental import pallas as pl
from jax.experimental.pallas import tpu as pltpu
from jax.sharding import PartitionSpec as P

BLOCK = 256
EACH = 2
OUTER_FLOPS = 4 << 30
PROJECT_VMEM = 16 << 20
SMALL_VMEM = 8 << 20
ROWS = 4
ROW_ORDER = (0, 2, 3, 1)
NO_COST = pl.CostEstimate(flops=0, bytes_accessed=0, transcendentals=0)
HIGHEST = lax.Precision.HIGHEST


def nt_dot(a, b, precision=None):
    return lax.dot_general(
        a, b, (((1,), (1,)), ((), ())), preferred_element_type=jnp.float32, precision=precision
    )


def project_block(hidden, grad, w):
    width = hidden.shape[1]
    return nt_dot(hidden, w[:, :width]) + nt_dot(grad, w[:, width:])


def theirs_kernel(n, core_ref, chip_ref, hidden_ref, grad_ref, pin_ref, pout_ref, *refs):
    outs, (own_hidden, own_grad, w_ref, hidden, grad, sem, w_sem) = refs[:-7], refs[-7:]
    rank, width = pin_ref.shape
    depth = pout_ref.shape[1]
    weights = [
        pltpu.make_async_copy(pin_ref, w_ref.at[pl.ds(0, rank), pl.ds(0, width)], w_sem.at[0]),
        pltpu.make_async_copy(pout_ref, w_ref.at[pl.ds(rank, rank), pl.ds(width, depth)], w_sem.at[1]),
    ]
    copies = []
    for j, (half, buffers) in enumerate(((1 - core_ref[0], (hidden, grad)), (core_ref[0], (own_hidden, own_grad)))):
        for k in range(n):
            first = (half * n + jnp.bitwise_xor(chip_ref[0], k)) * BLOCK
            rows = pl.ds(pl.multiple_of(first, BLOCK), BLOCK)
            for i, (source, buffer) in enumerate(zip((hidden_ref, grad_ref), buffers)):
                copies.append(
                    pltpu.make_async_copy(source.at[rows, :], buffer.at[pl.ds(k * BLOCK, BLOCK), :], sem.at[j, k, i])
                )
    for copy in weights + copies[: 2 * n]:
        copy.start()
    w_ref[rank:, :width] = jnp.zeros((rank, width), w_ref.dtype)
    w_ref[:rank, width:] = jnp.zeros((rank, depth), w_ref.dtype)
    for copy in weights:
        copy.wait()
    for copy in copies[2 * n :]:
        copy.start()
    for copy in copies[: 2 * n]:
        copy.wait()
    for k in range(n):
        rows = pl.ds(k * BLOCK, BLOCK)
        outs[k // EACH][pl.ds(k % EACH * BLOCK, BLOCK), :] = project_block(hidden[rows, :], grad[rows, :], w_ref)
    for copy in copies[2 * n :]:
        copy.wait()


def project_theirs(core, chip, hidden, grad, pin_t, pout_t):
    rank, width = pin_t.shape
    depth = pout_t.shape[1]
    half = hidden.shape[0] // 2
    n = half // BLOCK
    messages = n // EACH
    vmem = pl.BlockSpec(memory_space=pltpu.VMEM)
    hbm = pl.BlockSpec(memory_space=pltpu.HBM)
    held = [pltpu.with_memory_space_constraint(x, pltpu.HBM) for x in (hidden, grad, pin_t, pout_t)]
    outs = pl.pallas_call(
        functools.partial(theirs_kernel, n),
        out_shape=[jax.ShapeDtypeStruct((EACH * BLOCK, 2 * rank), jnp.float32)] * messages
        + [
            pltpu.VMEM((half, width), hidden.dtype),
            pltpu.VMEM((half, depth), grad.dtype),
            pltpu.VMEM((2 * rank, width + depth), pin_t.dtype),
        ],
        in_specs=[pl.BlockSpec(memory_space=pltpu.SMEM)] * 2 + [hbm] * 4,
        out_specs=[vmem] * (messages + 3),
        scratch_shapes=[
            pltpu.VMEM((half, width), hidden.dtype),
            pltpu.VMEM((half, depth), grad.dtype),
            pltpu.SemaphoreType.DMA((2, n, 2)),
            pltpu.SemaphoreType.DMA((2,)),
        ],
        compiler_params=pltpu.CompilerParams(vmem_limit_bytes=PROJECT_VMEM),
        cost_estimate=NO_COST,
        name="project_theirs",
    )(core[None], chip[None], *held)
    return outs[:messages], outs[messages:]


def mine_kernel(hidden_ref, grad_ref, w_ref, *outs):
    for k, out in enumerate(outs):
        rows = pl.ds(k * BLOCK, BLOCK)
        out[...] = project_block(hidden_ref[rows, :], grad_ref[rows, :], w_ref)


def project_mine(hidden, grad, w):
    n = hidden.shape[0] // BLOCK
    vmem = pl.BlockSpec(memory_space=pltpu.VMEM)
    held = [pltpu.with_memory_space_constraint(x, pltpu.VMEM) for x in (hidden, grad, w)]
    return pl.pallas_call(
        mine_kernel,
        out_shape=[jax.ShapeDtypeStruct((BLOCK, w.shape[0]), jnp.float32)] * n,
        in_specs=[vmem] * 3,
        out_specs=[vmem] * n,
        compiler_params=pltpu.CompilerParams(vmem_limit_bytes=SMALL_VMEM),
        cost_estimate=NO_COST,
        name="project_mine",
    )(*held)


def pair_kernel(n, *refs):
    mine, arrived, outs = refs[:n], refs[n:-n], refs[-n:]
    for k, out in enumerate(outs):
        out[...] = mine[k][...] + arrived[k // EACH][pl.ds(k % EACH * BLOCK, BLOCK), :]


def pair_sum(mine, arrived):
    vmem = pl.BlockSpec(memory_space=pltpu.VMEM)
    return pl.pallas_call(
        functools.partial(pair_kernel, len(mine)),
        out_shape=[jax.ShapeDtypeStruct(x.shape, x.dtype) for x in mine],
        in_specs=[vmem] * (len(mine) + len(arrived)),
        out_specs=[vmem] * len(mine),
        compiler_params=pltpu.CompilerParams(vmem_limit_bytes=SMALL_VMEM),
        cost_estimate=NO_COST,
        name="pair_sum",
    )(*mine, *arrived)


def outer_kernel(block_ref, row_ref, mask_ref, *refs):
    parts, (out_ref, tmp_ref, both_ref) = refs[:-3], refs[-3:]
    mask = mask_ref[pl.ds(block_ref[0], 1), :].astype(jnp.float32)
    total = functools.reduce(lambda a, b: a + b, [r[...] for r in parts])
    rank = total.shape[1] // 2
    masked = total.T[rank:, :] * mask
    tmp_ref[:rank, :] = lax.dot_general(
        masked, total, (((1,), (0,)), ((), ())), preferred_element_type=jnp.float32, precision=HIGHEST
    )
    even = tmp_ref[pl.ds(0, rank // 2, stride=2), :]
    odd = tmp_ref[pl.ds(1, rank // 2, stride=2), :]
    both_ref[: rank // 2, :] = jnp.concatenate([even[:, :rank], odd[:, :rank]], axis=1)
    layers = out_ref.shape[0] // ROWS
    for k, other in enumerate(ROW_ORDER):
        row = jnp.bitwise_xor(row_ref[0], other)
        out_ref[pl.ds(k * layers, layers), :] = both_ref[pl.ds(row, layers, stride=ROWS), :]


def outer(block, y, mask, parts):
    vmem = pl.BlockSpec(memory_space=pltpu.VMEM)
    rank = parts[0].shape[1] // 2
    return pl.pallas_call(
        outer_kernel,
        out_shape=jax.ShapeDtypeStruct((rank // 2, 2 * rank), jnp.float32),
        in_specs=[pl.BlockSpec(memory_space=pltpu.SMEM)] * 2 + [vmem] * (1 + len(parts)),
        out_specs=vmem,
        scratch_shapes=[pltpu.VMEM((n + 8, 2 * rank), jnp.float32) for n in (rank, rank // 2)],
        compiler_params=pltpu.CompilerParams(vmem_limit_bytes=SMALL_VMEM),
        cost_estimate=pl.CostEstimate(flops=OUTER_FLOPS, bytes_accessed=0, transcendentals=0),
        name="outer",
    )(block[None], y[None], mask, *parts)


def sum_kernel(*refs):
    refs[-1][...] = functools.reduce(lambda a, b: a + b, [r[...] for r in refs[:-1]])


def sum_parts(parts):
    vmem = pl.BlockSpec(memory_space=pltpu.VMEM)
    return pl.pallas_call(
        sum_kernel,
        out_shape=jax.ShapeDtypeStruct(parts[0].shape, jnp.float32),
        in_specs=[vmem] * len(parts),
        out_specs=vmem,
        compiler_params=pltpu.CompilerParams(vmem_limit_bytes=SMALL_VMEM),
        cost_estimate=NO_COST,
        name="sum_parts",
    )(*parts)


def add_blocks(dots, squares, unit, q_ref):
    for z in range(q_ref.shape[0]):
        q = q_ref[z].astype(jnp.float32)
        dots += q * unit[z : z + 1, :]
        squares += q * q
    return dots, squares


def start_kernel(a_ref, b_ref, *refs):
    q_refs, (last_ref, dots_ref, squares_ref) = refs[:-3], refs[-3:]
    grad = a_ref[...] + b_ref[...]
    mean = jnp.sum(grad * grad, keepdims=True) / grad.size
    unit = (grad / jnp.sqrt(mean + 1e-06)).astype(jnp.bfloat16).astype(jnp.float32)
    layers = q_refs[0].shape[0]
    dots = squares = jnp.zeros(dots_ref.shape, jnp.float32)
    for k, q_ref in enumerate(q_refs):
        dots, squares = add_blocks(dots, squares, unit[k * layers : (k + 1) * layers, :], q_ref)
    dots_ref[...] = dots
    squares_ref[...] = squares
    last_ref[...] = unit[len(q_refs) * layers :, :]


def score_start(parts, q):
    vmem = pl.BlockSpec(memory_space=pltpu.VMEM)
    layers, qlocal, lanes = q[0].shape
    sums = jax.ShapeDtypeStruct((qlocal, lanes), jnp.float32)
    return pl.pallas_call(
        start_kernel,
        out_shape=[jax.ShapeDtypeStruct((layers, lanes), jnp.float32), sums, sums],
        in_specs=[vmem] * (len(parts) + len(q)),
        out_specs=[vmem] * 3,
        compiler_params=pltpu.CompilerParams(vmem_limit_bytes=SMALL_VMEM),
        cost_estimate=NO_COST,
        name="score_start",
    )(*parts, *q)


def score_kernel(entries, factor_ref, unit_ref, dots_ref, squares_ref, q_ref, out_ref):
    dots, squares = add_blocks(dots_ref[...], squares_ref[...], unit_ref, q_ref)
    dots, squares = [jnp.sum(x.T, axis=0, keepdims=True) for x in (dots, squares)]
    scores = dots / jnp.sqrt(squares / entries + 1e-06)
    out_ref[...] = jnp.where(factor_ref[...] == 0.0, 0.0, scores * factor_ref[...])


def score(entries, factor, started, q):
    vmem = pl.BlockSpec(memory_space=pltpu.VMEM)
    return pl.pallas_call(
        functools.partial(score_kernel, entries),
        out_shape=jax.ShapeDtypeStruct((1, q.shape[1]), jnp.float32),
        in_specs=[vmem] * 5,
        out_specs=vmem,
        compiler_params=pltpu.CompilerParams(vmem_limit_bytes=SMALL_VMEM),
        cost_estimate=NO_COST,
        name="score",
    )(factor, *started, q)


def hops(k):
    return 2 if k == 2 else 1


def body(hidden_in, out_grad, proj_in, proj_out, token_mask, cand_ids, queries):
    rank = proj_in.shape[1]
    devices = lax.axis_size("tensor")
    chips = devices // 2
    dp = lax.axis_size("dp")
    me = lax.axis_index("tensor").astype(jnp.int32)
    core, chip = me % 2, me // 2
    qlocal, qcols = queries.shape

    def swap(x, mask):
        return lax.ppermute(x, "tensor", [(i, i ^ mask) for i in range(devices)])

    with jax.named_scope("gather_queries"):
        layers = dp // ROWS
        columns = [[z * ROWS + y for z in range(layers)] for y in range(ROWS)]
        copies = jnp.broadcast_to(queries[None], (layers, *queries.shape))
        column = lax.all_to_all(copies, "dp", 0, 0, tiled=True, axis_index_groups=columns)
        gathered = [column] + [lax.ppermute(column, "dp", [(i, i ^ k) for i in range(dp)]) for k in ROW_ORDER[1:]]

    with jax.named_scope("project"):
        theirs, kept = project_theirs(core, chip, hidden_in, out_grad, proj_in.T, proj_out.T)
        arrived = [swap(part, 1) for part in theirs]
        mine = project_mine(*kept)
    with jax.named_scope("exchange_tokens"):
        blocks = pair_sum(mine, arrived)
        order = sorted(range(1, chips), key=lambda k: (-hops(k), -k))
        parts = [blocks[0]] + [swap(blocks[k], 2 * k) for k in order]
    with jax.named_scope("outer"):
        row = lax.axis_index("dp").astype(jnp.int32) % ROWS
        partial = outer(core * chips + chip, row, token_mask.reshape(-1, BLOCK), parts)
    with jax.named_scope("exchange_grad"):
        pair = sum_parts([partial, swap(partial, 1)])
        four = sum_parts([pair, swap(pair, 6)])
        partials = [four, swap(four, 2)]
    with jax.named_scope("score"):
        index = me * qlocal + jnp.arange(qlocal, dtype=jnp.int32)
        factor = jnp.where(index[None, :] == cand_ids[:, None], jnp.float32(0.0), jnp.float32(1.0 / rank))
        return score(rank * rank, factor, score_start(partials, gathered[:-1]), gathered[-1])


def solution(mesh):
    placed = (
        P("dp", "tensor"),
        P("dp", "tensor"),
        P("tensor", None),
        P("tensor", None),
        P("dp"),
        P("dp"),
        P("tensor", "dp"),
    )
    return jax.shard_map(
        body, mesh=mesh, in_specs=placed, out_specs=P("dp", "tensor"), check_vma=False
    )
```

```python
import functools

import jax
import jax.numpy as jnp
from jax import lax
from jax.experimental import pallas as pl
from jax.experimental.pallas import tpu as pltpu
from jax.sharding import PartitionSpec as P

BLOCK = 256
EACH = 2
OUTER_FLOPS = 4 << 30
PROJECT_VMEM = 16 << 20
SMALL_VMEM = 8 << 20
ROWS = 4
ROW_ORDER = (0, 2, 3, 1)
NO_COST = pl.CostEstimate(flops=0, bytes_accessed=0, transcendentals=0)
HIGHEST = lax.Precision.HIGHEST


def nt_dot(a, b, precision=None):
    return lax.dot_general(
        a, b, (((1,), (1,)), ((), ())), preferred_element_type=jnp.float32, precision=precision
    )


def project_block(hidden, grad, w):
    width = hidden.shape[1]
    return nt_dot(hidden, w[:, :width]) + nt_dot(grad, w[:, width:])


def theirs_kernel(n, core_ref, chip_ref, hidden_ref, grad_ref, pin_ref, pout_ref, *refs):
    outs, (own_hidden, own_grad, w_ref, hidden, grad, sem, w_sem) = refs[:-7], refs[-7:]
    rank, width = pin_ref.shape
    depth = pout_ref.shape[1]
    weights = [
        pltpu.make_async_copy(pin_ref, w_ref.at[pl.ds(0, rank), pl.ds(0, width)], w_sem.at[0]),
        pltpu.make_async_copy(pout_ref, w_ref.at[pl.ds(rank, rank), pl.ds(width, depth)], w_sem.at[1]),
    ]
    copies = []
    for j, (half, buffers) in enumerate(((1 - core_ref[0], (hidden, grad)), (core_ref[0], (own_hidden, own_grad)))):
        for k in range(n):
            first = (half * n + jnp.bitwise_xor(chip_ref[0], k)) * BLOCK
            rows = pl.ds(pl.multiple_of(first, BLOCK), BLOCK)
            for i, (source, buffer) in enumerate(zip((hidden_ref, grad_ref), buffers)):
                copies.append(
                    pltpu.make_async_copy(source.at[rows, :], buffer.at[pl.ds(k * BLOCK, BLOCK), :], sem.at[j, k, i])
                )
    for copy in weights + copies[: 2 * n]:
        copy.start()
    w_ref[rank:, :width] = jnp.zeros((rank, width), w_ref.dtype)
    w_ref[:rank, width:] = jnp.zeros((rank, depth), w_ref.dtype)
    for copy in weights:
        copy.wait()
    for copy in copies[2 * n :]:
        copy.start()
    for copy in copies[: 2 * n]:
        copy.wait()
    for k in range(n):
        rows = pl.ds(k * BLOCK, BLOCK)
        outs[k // EACH][pl.ds(k % EACH * BLOCK, BLOCK), :] = project_block(hidden[rows, :], grad[rows, :], w_ref)
    for copy in copies[2 * n :]:
        copy.wait()


def project_theirs(core, chip, hidden, grad, pin_t, pout_t):
    rank, width = pin_t.shape
    depth = pout_t.shape[1]
    half = hidden.shape[0] // 2
    n = half // BLOCK
    messages = n // EACH
    vmem = pl.BlockSpec(memory_space=pltpu.VMEM)
    hbm = pl.BlockSpec(memory_space=pltpu.HBM)
    held = [pltpu.with_memory_space_constraint(x, pltpu.HBM) for x in (hidden, grad, pin_t, pout_t)]
    outs = pl.pallas_call(
        functools.partial(theirs_kernel, n),
        out_shape=[jax.ShapeDtypeStruct((EACH * BLOCK, 2 * rank), jnp.float32)] * messages
        + [
            pltpu.VMEM((half, width), hidden.dtype),
            pltpu.VMEM((half, depth), grad.dtype),
            pltpu.VMEM((2 * rank, width + depth), pin_t.dtype),
        ],
        in_specs=[pl.BlockSpec(memory_space=pltpu.SMEM)] * 2 + [hbm] * 4,
        out_specs=[vmem] * (messages + 3),
        scratch_shapes=[
            pltpu.VMEM((half, width), hidden.dtype),
            pltpu.VMEM((half, depth), grad.dtype),
            pltpu.SemaphoreType.DMA((2, n, 2)),
            pltpu.SemaphoreType.DMA((2,)),
        ],
        compiler_params=pltpu.CompilerParams(vmem_limit_bytes=PROJECT_VMEM),
        cost_estimate=NO_COST,
        name="project_theirs",
    )(core[None], chip[None], *held)
    return outs[:messages], outs[messages:]


def mine_kernel(hidden_ref, grad_ref, w_ref, *outs):
    for k, out in enumerate(outs):
        rows = pl.ds(k * BLOCK, BLOCK)
        out[...] = project_block(hidden_ref[rows, :], grad_ref[rows, :], w_ref)


def project_mine(hidden, grad, w):
    n = hidden.shape[0] // BLOCK
    vmem = pl.BlockSpec(memory_space=pltpu.VMEM)
    held = [pltpu.with_memory_space_constraint(x, pltpu.VMEM) for x in (hidden, grad, w)]
    return pl.pallas_call(
        mine_kernel,
        out_shape=[jax.ShapeDtypeStruct((BLOCK, w.shape[0]), jnp.float32)] * n,
        in_specs=[vmem] * 3,
        out_specs=[vmem] * n,
        compiler_params=pltpu.CompilerParams(vmem_limit_bytes=SMALL_VMEM),
        cost_estimate=NO_COST,
        name="project_mine",
    )(*held)


def pair_kernel(n, *refs):
    mine, arrived, outs = refs[:n], refs[n:-n], refs[-n:]
    for k, out in enumerate(outs):
        out[...] = mine[k][...] + arrived[k // EACH][pl.ds(k % EACH * BLOCK, BLOCK), :]


def pair_sum(mine, arrived):
    vmem = pl.BlockSpec(memory_space=pltpu.VMEM)
    return pl.pallas_call(
        functools.partial(pair_kernel, len(mine)),
        out_shape=[jax.ShapeDtypeStruct(x.shape, x.dtype) for x in mine],
        in_specs=[vmem] * (len(mine) + len(arrived)),
        out_specs=[vmem] * len(mine),
        compiler_params=pltpu.CompilerParams(vmem_limit_bytes=SMALL_VMEM),
        cost_estimate=NO_COST,
        name="pair_sum",
    )(*mine, *arrived)


def outer_kernel(block_ref, row_ref, mask_ref, *refs):
    parts, (out_ref, tmp_ref, both_ref) = refs[:-3], refs[-3:]
    mask = mask_ref[pl.ds(block_ref[0], 1), :].astype(jnp.float32)
    total = functools.reduce(lambda a, b: a + b, [r[...] for r in parts])
    rank = total.shape[1] // 2
    masked = total.T[rank:, :] * mask
    tmp_ref[:rank, :] = lax.dot_general(
        masked, total, (((1,), (0,)), ((), ())), preferred_element_type=jnp.float32, precision=HIGHEST
    )
    even = tmp_ref[pl.ds(0, rank // 2, stride=2), :]
    odd = tmp_ref[pl.ds(1, rank // 2, stride=2), :]
    both_ref[: rank // 2, :] = jnp.concatenate([even[:, :rank], odd[:, :rank]], axis=1)
    layers = out_ref.shape[0] // ROWS
    for k, other in enumerate(ROW_ORDER):
        row = jnp.bitwise_xor(row_ref[0], other)
        out_ref[pl.ds(k * layers, layers), :] = both_ref[pl.ds(row, layers, stride=ROWS), :]


def outer(block, y, mask, parts):
    vmem = pl.BlockSpec(memory_space=pltpu.VMEM)
    rank = parts[0].shape[1] // 2
    return pl.pallas_call(
        outer_kernel,
        out_shape=jax.ShapeDtypeStruct((rank // 2, 2 * rank), jnp.float32),
        in_specs=[pl.BlockSpec(memory_space=pltpu.SMEM)] * 2 + [vmem] * (1 + len(parts)),
        out_specs=vmem,
        scratch_shapes=[pltpu.VMEM((n + 8, 2 * rank), jnp.float32) for n in (rank, rank // 2)],
        compiler_params=pltpu.CompilerParams(vmem_limit_bytes=SMALL_VMEM),
        cost_estimate=pl.CostEstimate(flops=OUTER_FLOPS, bytes_accessed=0, transcendentals=0),
        name="outer",
    )(block[None], y[None], mask, *parts)


def sum_kernel(*refs):
    refs[-1][...] = functools.reduce(lambda a, b: a + b, [r[...] for r in refs[:-1]])


def sum_parts(parts):
    vmem = pl.BlockSpec(memory_space=pltpu.VMEM)
    return pl.pallas_call(
        sum_kernel,
        out_shape=jax.ShapeDtypeStruct(parts[0].shape, jnp.float32),
        in_specs=[vmem] * len(parts),
        out_specs=vmem,
        compiler_params=pltpu.CompilerParams(vmem_limit_bytes=SMALL_VMEM),
        cost_estimate=NO_COST,
        name="sum_parts",
    )(*parts)


def after_kernel(x_ref, _, out_ref):
    out_ref[...] = x_ref[...]


def after(x, other):
    vmem = pl.BlockSpec(memory_space=pltpu.VMEM)
    return pl.pallas_call(
        after_kernel,
        out_shape=jax.ShapeDtypeStruct(x.shape, x.dtype),
        in_specs=[vmem, pl.BlockSpec(memory_space=pl.ANY)],
        out_specs=vmem,
        compiler_params=pltpu.CompilerParams(vmem_limit_bytes=SMALL_VMEM),
        cost_estimate=NO_COST,
        name="after",
    )(x, other)


def add_blocks(dots, squares, unit, q_ref):
    for z in range(q_ref.shape[0]):
        q = q_ref[z].astype(jnp.float32)
        dots += q * unit[z : z + 1, :]
        squares += q * q
    return dots, squares


def start_kernel(a_ref, b_ref, *refs):
    q_refs, (last_ref, dots_ref, squares_ref) = refs[:-3], refs[-3:]
    grad = a_ref[...] + b_ref[...]
    mean = jnp.sum(grad * grad, keepdims=True) / grad.size
    unit = (grad / jnp.sqrt(mean + 1e-06)).astype(jnp.bfloat16).astype(jnp.float32)
    layers = q_refs[0].shape[0]
    dots = squares = jnp.zeros(dots_ref.shape, jnp.float32)
    for k, q_ref in enumerate(q_refs):
        dots, squares = add_blocks(dots, squares, unit[k * layers : (k + 1) * layers, :], q_ref)
    dots_ref[...] = dots
    squares_ref[...] = squares
    last_ref[...] = unit[len(q_refs) * layers :, :]


def score_start(parts, q):
    vmem = pl.BlockSpec(memory_space=pltpu.VMEM)
    layers, qlocal, lanes = q[0].shape
    sums = jax.ShapeDtypeStruct((qlocal, lanes), jnp.float32)
    return pl.pallas_call(
        start_kernel,
        out_shape=[jax.ShapeDtypeStruct((layers, lanes), jnp.float32), sums, sums],
        in_specs=[vmem] * (len(parts) + len(q)),
        out_specs=[vmem] * 3,
        compiler_params=pltpu.CompilerParams(vmem_limit_bytes=SMALL_VMEM),
        cost_estimate=NO_COST,
        name="score_start",
    )(*parts, *q)


def score_kernel(entries, factor_ref, unit_ref, dots_ref, squares_ref, q_ref, out_ref):
    dots, squares = add_blocks(dots_ref[...], squares_ref[...], unit_ref, q_ref)
    dots, squares = [jnp.sum(x.T, axis=0, keepdims=True) for x in (dots, squares)]
    scores = dots / jnp.sqrt(squares / entries + 1e-06)
    out_ref[...] = jnp.where(factor_ref[...] == 0.0, 0.0, scores * factor_ref[...])


def score(entries, factor, started, q):
    vmem = pl.BlockSpec(memory_space=pltpu.VMEM)
    return pl.pallas_call(
        functools.partial(score_kernel, entries),
        out_shape=jax.ShapeDtypeStruct((1, q.shape[1]), jnp.float32),
        in_specs=[vmem] * 5,
        out_specs=vmem,
        compiler_params=pltpu.CompilerParams(vmem_limit_bytes=SMALL_VMEM),
        cost_estimate=NO_COST,
        name="score",
    )(factor, *started, q)


def hops(k):
    return 2 if k == 2 else 1


def body(hidden_in, out_grad, proj_in, proj_out, token_mask, cand_ids, queries):
    rank = proj_in.shape[1]
    devices = lax.axis_size("tensor")
    chips = devices // 2
    dp = lax.axis_size("dp")
    me = lax.axis_index("tensor").astype(jnp.int32)
    core, chip = me % 2, me // 2
    qlocal, qcols = queries.shape

    def swap(x, mask):
        return lax.ppermute(x, "tensor", [(i, i ^ mask) for i in range(devices)])

    with jax.named_scope("gather_queries"):
        layers = dp // ROWS
        columns = [[z * ROWS + y for z in range(layers)] for y in range(ROWS)]
        copies = jnp.broadcast_to(queries[None], (layers, *queries.shape))
        column = lax.all_to_all(copies, "dp", 0, 0, tiled=True, axis_index_groups=columns)
        gathered = [column] + [lax.ppermute(column, "dp", [(i, i ^ k) for i in range(dp)]) for k in ROW_ORDER[1:]]

    with jax.named_scope("project"):
        theirs, kept = project_theirs(core, chip, hidden_in, out_grad, proj_in.T, proj_out.T)
        arrived = [swap(part, 1) for part in theirs]
        mine = project_mine(*kept)
    with jax.named_scope("exchange_tokens"):
        blocks = pair_sum(mine, arrived)
        order = sorted(range(1, chips), key=lambda k: (-hops(k), -k))
        parts = [blocks[0]] + [swap(blocks[k], 2 * k) for k in order]
    with jax.named_scope("outer"):
        row = lax.axis_index("dp").astype(jnp.int32) % ROWS
        partial = outer(core * chips + chip, row, token_mask.reshape(-1, BLOCK), parts)
    with jax.named_scope("exchange_grad"):
        pair = sum_parts([partial, swap(partial, 1)])
        third = after(pair, gathered[1])
        partials = [sum_parts([pair, swap(pair, 4), swap(pair, 6)]), swap(third, 2)]
    with jax.named_scope("score"):
        index = me * qlocal + jnp.arange(qlocal, dtype=jnp.int32)
        factor = jnp.where(index[None, :] == cand_ids[:, None], jnp.float32(0.0), jnp.float32(1.0 / rank))
        return score(rank * rank, factor, score_start(partials, gathered[:-1]), gathered[-1])


def solution(mesh):
    placed = (
        P("dp", "tensor"),
        P("dp", "tensor"),
        P("tensor", None),
        P("tensor", None),
        P("dp"),
        P("dp"),
        P("tensor", "dp"),
    )
    return jax.shard_map(
        body, mesh=mesh, in_specs=placed, out_specs=P("dp", "tensor"), check_vma=False
    )
```

```python
import functools

import jax
import jax.numpy as jnp
from jax import lax
from jax.experimental import pallas as pl
from jax.experimental.pallas import tpu as pltpu
from jax.sharding import PartitionSpec as P

BLOCK = 256
EACH = 2
OUTER_FLOPS = 4 << 30
PROJECT_VMEM = 16 << 20
SMALL_VMEM = 8 << 20
ROWS = 4
ROW_ORDER = (0, 2, 3, 1)
NO_COST = pl.CostEstimate(flops=0, bytes_accessed=0, transcendentals=0)
HIGHEST = lax.Precision.HIGHEST


def nt_dot(a, b, precision=None):
    return lax.dot_general(
        a, b, (((1,), (1,)), ((), ())), preferred_element_type=jnp.float32, precision=precision
    )


def project_block(hidden, grad, w):
    width = hidden.shape[1]
    return nt_dot(hidden, w[:, :width]) + nt_dot(grad, w[:, width:])


def theirs_kernel(n, core_ref, chip_ref, hidden_ref, grad_ref, pin_ref, pout_ref, *refs):
    outs, (own_hidden, own_grad, w_ref, hidden, grad, sem, w_sem) = refs[:-7], refs[-7:]
    rank, width = pin_ref.shape
    depth = pout_ref.shape[1]
    weights = [
        pltpu.make_async_copy(pin_ref, w_ref.at[pl.ds(0, rank), pl.ds(0, width)], w_sem.at[0]),
        pltpu.make_async_copy(pout_ref, w_ref.at[pl.ds(rank, rank), pl.ds(width, depth)], w_sem.at[1]),
    ]
    copies = []
    for j, (half, buffers) in enumerate(((1 - core_ref[0], (hidden, grad)), (core_ref[0], (own_hidden, own_grad)))):
        for k in range(n):
            first = (half * n + jnp.bitwise_xor(chip_ref[0], k)) * BLOCK
            rows = pl.ds(pl.multiple_of(first, BLOCK), BLOCK)
            for i, (source, buffer) in enumerate(zip((hidden_ref, grad_ref), buffers)):
                copies.append(
                    pltpu.make_async_copy(source.at[rows, :], buffer.at[pl.ds(k * BLOCK, BLOCK), :], sem.at[j, k, i])
                )
    for copy in weights + copies[: 2 * n]:
        copy.start()
    w_ref[rank:, :width] = jnp.zeros((rank, width), w_ref.dtype)
    w_ref[:rank, width:] = jnp.zeros((rank, depth), w_ref.dtype)
    for copy in weights:
        copy.wait()
    for copy in copies[2 * n :]:
        copy.start()
    for copy in copies[: 2 * n]:
        copy.wait()
    for k in range(n):
        rows = pl.ds(k * BLOCK, BLOCK)
        outs[k // EACH][pl.ds(k % EACH * BLOCK, BLOCK), :] = project_block(hidden[rows, :], grad[rows, :], w_ref)
    for copy in copies[2 * n :]:
        copy.wait()


def project_theirs(core, chip, hidden, grad, pin_t, pout_t):
    rank, width = pin_t.shape
    depth = pout_t.shape[1]
    half = hidden.shape[0] // 2
    n = half // BLOCK
    messages = n // EACH
    vmem = pl.BlockSpec(memory_space=pltpu.VMEM)
    hbm = pl.BlockSpec(memory_space=pltpu.HBM)
    held = [pltpu.with_memory_space_constraint(x, pltpu.HBM) for x in (hidden, grad, pin_t, pout_t)]
    outs = pl.pallas_call(
        functools.partial(theirs_kernel, n),
        out_shape=[jax.ShapeDtypeStruct((EACH * BLOCK, 2 * rank), jnp.float32)] * messages
        + [
            pltpu.VMEM((half, width), hidden.dtype),
            pltpu.VMEM((half, depth), grad.dtype),
            pltpu.VMEM((2 * rank, width + depth), pin_t.dtype),
        ],
        in_specs=[pl.BlockSpec(memory_space=pltpu.SMEM)] * 2 + [hbm] * 4,
        out_specs=[vmem] * (messages + 3),
        scratch_shapes=[
            pltpu.VMEM((half, width), hidden.dtype),
            pltpu.VMEM((half, depth), grad.dtype),
            pltpu.SemaphoreType.DMA((2, n, 2)),
            pltpu.SemaphoreType.DMA((2,)),
        ],
        compiler_params=pltpu.CompilerParams(vmem_limit_bytes=PROJECT_VMEM),
        cost_estimate=NO_COST,
        name="project_theirs",
    )(core[None], chip[None], *held)
    return outs[:messages], outs[messages:]


def mine_kernel(hidden_ref, grad_ref, w_ref, *outs):
    for k, out in enumerate(outs):
        rows = pl.ds(k * BLOCK, BLOCK)
        out[...] = project_block(hidden_ref[rows, :], grad_ref[rows, :], w_ref)


def project_mine(hidden, grad, w):
    n = hidden.shape[0] // BLOCK
    vmem = pl.BlockSpec(memory_space=pltpu.VMEM)
    held = [pltpu.with_memory_space_constraint(x, pltpu.VMEM) for x in (hidden, grad, w)]
    return pl.pallas_call(
        mine_kernel,
        out_shape=[jax.ShapeDtypeStruct((BLOCK, w.shape[0]), jnp.float32)] * n,
        in_specs=[vmem] * 3,
        out_specs=[vmem] * n,
        compiler_params=pltpu.CompilerParams(vmem_limit_bytes=SMALL_VMEM),
        cost_estimate=NO_COST,
        name="project_mine",
    )(*held)


def pair_kernel(n, *refs):
    mine, arrived, outs = refs[:n], refs[n:-n], refs[-n:]
    for k, out in enumerate(outs):
        out[...] = mine[k][...] + arrived[k // EACH][pl.ds(k % EACH * BLOCK, BLOCK), :]


def pair_sum(mine, arrived):
    vmem = pl.BlockSpec(memory_space=pltpu.VMEM)
    return pl.pallas_call(
        functools.partial(pair_kernel, len(mine)),
        out_shape=[jax.ShapeDtypeStruct(x.shape, x.dtype) for x in mine],
        in_specs=[vmem] * (len(mine) + len(arrived)),
        out_specs=[vmem] * len(mine),
        compiler_params=pltpu.CompilerParams(vmem_limit_bytes=SMALL_VMEM),
        cost_estimate=NO_COST,
        name="pair_sum",
    )(*mine, *arrived)


def outer_kernel(block_ref, row_ref, mask_ref, *refs):
    parts, (out_ref, tmp_ref, both_ref) = refs[:-3], refs[-3:]
    mask = mask_ref[pl.ds(block_ref[0], 1), :].astype(jnp.float32)
    total = functools.reduce(lambda a, b: a + b, [r[...] for r in parts])
    rank = total.shape[1] // 2
    masked = total.T[rank:, :] * mask
    tmp_ref[:rank, :] = lax.dot_general(
        masked, total, (((1,), (0,)), ((), ())), preferred_element_type=jnp.float32, precision=HIGHEST
    )
    even = tmp_ref[pl.ds(0, rank // 2, stride=2), :]
    odd = tmp_ref[pl.ds(1, rank // 2, stride=2), :]
    both_ref[: rank // 2, :] = jnp.concatenate([even[:, :rank], odd[:, :rank]], axis=1)
    layers = out_ref.shape[0] // ROWS
    for k, other in enumerate(ROW_ORDER):
        row = jnp.bitwise_xor(row_ref[0], other)
        out_ref[pl.ds(k * layers, layers), :] = both_ref[pl.ds(row, layers, stride=ROWS), :]


def outer(block, y, mask, parts):
    vmem = pl.BlockSpec(memory_space=pltpu.VMEM)
    rank = parts[0].shape[1] // 2
    return pl.pallas_call(
        outer_kernel,
        out_shape=jax.ShapeDtypeStruct((rank // 2, 2 * rank), jnp.float32),
        in_specs=[pl.BlockSpec(memory_space=pltpu.SMEM)] * 2 + [vmem] * (1 + len(parts)),
        out_specs=vmem,
        scratch_shapes=[pltpu.VMEM((n + 8, 2 * rank), jnp.float32) for n in (rank, rank // 2)],
        compiler_params=pltpu.CompilerParams(vmem_limit_bytes=SMALL_VMEM),
        cost_estimate=pl.CostEstimate(flops=OUTER_FLOPS, bytes_accessed=0, transcendentals=0),
        name="outer",
    )(block[None], y[None], mask, *parts)


def sum_kernel(*refs):
    refs[-1][...] = functools.reduce(lambda a, b: a + b, [r[...] for r in refs[:-1]])


def sum_parts(parts):
    vmem = pl.BlockSpec(memory_space=pltpu.VMEM)
    return pl.pallas_call(
        sum_kernel,
        out_shape=jax.ShapeDtypeStruct(parts[0].shape, jnp.float32),
        in_specs=[vmem] * len(parts),
        out_specs=vmem,
        compiler_params=pltpu.CompilerParams(vmem_limit_bytes=SMALL_VMEM),
        cost_estimate=NO_COST,
        name="sum_parts",
    )(*parts)


def after_kernel(x_ref, _, out_ref):
    out_ref[...] = x_ref[...]


def after(x, other):
    vmem = pl.BlockSpec(memory_space=pltpu.VMEM)
    return pl.pallas_call(
        after_kernel,
        out_shape=jax.ShapeDtypeStruct(x.shape, x.dtype),
        in_specs=[vmem, pl.BlockSpec(memory_space=pl.ANY)],
        out_specs=vmem,
        compiler_params=pltpu.CompilerParams(vmem_limit_bytes=SMALL_VMEM),
        cost_estimate=NO_COST,
        name="after",
    )(x, other)


def add_blocks(dots, squares, unit, q_ref):
    for z in range(q_ref.shape[0]):
        q = q_ref[z].astype(jnp.float32)
        dots += q * unit[z : z + 1, :]
        squares += q * q
    return dots, squares


def start_kernel(n, *refs):
    parts, q_refs, (last_ref, dots_ref, squares_ref) = refs[:n], refs[n:-3], refs[-3:]
    grad = functools.reduce(lambda a, b: a + b, [r[...] for r in parts])
    mean = jnp.sum(grad * grad, keepdims=True) / grad.size
    unit = (grad / jnp.sqrt(mean + 1e-06)).astype(jnp.bfloat16).astype(jnp.float32)
    layers = q_refs[0].shape[0]
    dots = squares = jnp.zeros(dots_ref.shape, jnp.float32)
    for k, q_ref in enumerate(q_refs):
        dots, squares = add_blocks(dots, squares, unit[k * layers : (k + 1) * layers, :], q_ref)
    dots_ref[...] = dots
    squares_ref[...] = squares
    last_ref[...] = unit[len(q_refs) * layers :, :]


def score_start(parts, q):
    vmem = pl.BlockSpec(memory_space=pltpu.VMEM)
    layers, qlocal, lanes = q[0].shape
    sums = jax.ShapeDtypeStruct((qlocal, lanes), jnp.float32)
    return pl.pallas_call(
        functools.partial(start_kernel, len(parts)),
        out_shape=[jax.ShapeDtypeStruct((layers, lanes), jnp.float32), sums, sums],
        in_specs=[vmem] * (len(parts) + len(q)),
        out_specs=[vmem] * 3,
        compiler_params=pltpu.CompilerParams(vmem_limit_bytes=SMALL_VMEM),
        cost_estimate=NO_COST,
        name="score_start",
    )(*parts, *q)


def score_kernel(entries, factor_ref, unit_ref, dots_ref, squares_ref, q_ref, out_ref):
    dots, squares = add_blocks(dots_ref[...], squares_ref[...], unit_ref, q_ref)
    dots, squares = [jnp.sum(x.T, axis=0, keepdims=True) for x in (dots, squares)]
    scores = dots / jnp.sqrt(squares / entries + 1e-06)
    out_ref[...] = jnp.where(factor_ref[...] == 0.0, 0.0, scores * factor_ref[...])


def score(entries, factor, started, q):
    vmem = pl.BlockSpec(memory_space=pltpu.VMEM)
    return pl.pallas_call(
        functools.partial(score_kernel, entries),
        out_shape=jax.ShapeDtypeStruct((1, q.shape[1]), jnp.float32),
        in_specs=[vmem] * 5,
        out_specs=vmem,
        compiler_params=pltpu.CompilerParams(vmem_limit_bytes=SMALL_VMEM),
        cost_estimate=NO_COST,
        name="score",
    )(factor, *started, q)


def hops(k):
    return 2 if k == 2 else 1


def body(hidden_in, out_grad, proj_in, proj_out, token_mask, cand_ids, queries):
    rank = proj_in.shape[1]
    devices = lax.axis_size("tensor")
    chips = devices // 2
    dp = lax.axis_size("dp")
    me = lax.axis_index("tensor").astype(jnp.int32)
    core, chip = me % 2, me // 2
    qlocal, qcols = queries.shape

    def swap(x, mask):
        return lax.ppermute(x, "tensor", [(i, i ^ mask) for i in range(devices)])

    with jax.named_scope("gather_queries"):
        layers = dp // ROWS
        columns = [[z * ROWS + y for z in range(layers)] for y in range(ROWS)]
        copies = jnp.broadcast_to(queries[None], (layers, *queries.shape))
        column = lax.all_to_all(copies, "dp", 0, 0, tiled=True, axis_index_groups=columns)
        gathered = [column] + [lax.ppermute(column, "dp", [(i, i ^ k) for i in range(dp)]) for k in ROW_ORDER[1:]]

    with jax.named_scope("project"):
        theirs, kept = project_theirs(core, chip, hidden_in, out_grad, proj_in.T, proj_out.T)
        arrived = [swap(part, 1) for part in theirs]
        mine = project_mine(*kept)
    with jax.named_scope("exchange_tokens"):
        blocks = pair_sum(mine, arrived)
        order = sorted(range(1, chips), key=lambda k: (-hops(k), -k))
        parts = [blocks[0]] + [swap(blocks[k], 2 * k) for k in order]
    with jax.named_scope("outer"):
        row = lax.axis_index("dp").astype(jnp.int32) % ROWS
        partial = outer(core * chips + chip, row, token_mask.reshape(-1, BLOCK), parts)
    with jax.named_scope("exchange_grad"):
        pair = sum_parts([partial, swap(partial, 1)])
        third = after(pair, gathered[1])
        partials = [pair, swap(pair, 6), swap(pair, 4), swap(third, 2)]
    with jax.named_scope("score"):
        index = me * qlocal + jnp.arange(qlocal, dtype=jnp.int32)
        factor = jnp.where(index[None, :] == cand_ids[:, None], jnp.float32(0.0), jnp.float32(1.0 / rank))
        return score(rank * rank, factor, score_start(partials, gathered[:-1]), gathered[-1])


def solution(mesh):
    placed = (
        P("dp", "tensor"),
        P("dp", "tensor"),
        P("tensor", None),
        P("tensor", None),
        P("dp"),
        P("dp"),
        P("tensor", "dp"),
    )
    return jax.shard_map(
        body, mesh=mesh, in_specs=placed, out_specs=P("dp", "tensor"), check_vma=False
    )
```
